32 devices in a mesh: groups: 2 (over x), seq: 16 (over z, y, core).
Axes of the slice: x: 2, y: 2, z: 4, core: 2. Of those that a mesh axis runs over, the one named last changes fastest.
Arguments:
- audio_stream: bfloat16 [64, 2048], P(('groups', 'seq')), parts along dimension 0, may hold values from -6 to 6
- audio_qkv: bfloat16 [3, 64, 2048], P(None, ('groups', 'seq')), parts along dimension 1, may hold values from -6 to 6
- video_qkv: bfloat16 [3, 4096, 2048], P(None, ('groups', 'seq')), parts along dimension 1, may hold values from -6 to 6
- attention_out: bfloat16 [2048, 2048], P('seq'), may hold values from -0.125 to 0.125
- norm_gain: float32 [2048], replicated, may hold values from 0.25 to 1.75
- weight_in: bfloat16 [2048, 8192], P(None, 'seq'), may hold values from -0.125 to 0.125
- weight_out: bfloat16 [8192, 2048], P('seq'), may hold values from -0.0625 to 0.0625
Outputs:
- video_mix: bfloat16 [4096, 2048], P(('groups', 'seq')), parts along dimension 0
- audio_result: bfloat16 [64, 2048], P(('groups', 'seq')), parts along dimension 0
The draws below stay inside these ranges and needn't reach their ends.
There are 2 independent parts, one for each index of `groups`. The reference program is written for one: setup_inputs(seed, part) draws one part's arguments, and reference() takes and returns one part's arrays. A program takes and returns all parts, laid end to end along the dimension named above; an argument that names none is the same for every part. Nothing has to cross between parts.
All inputs are finite; a program needn't handle non-finite values.
Results may differ from the reference program's by a relative error of at most 0.008.
Values may be sent and summed in bfloat16 or wider, within the bound.
A program may use at most 128 MiB of HBM per device.

```python
import math
import jax
import jax.numpy as jnp
from jax import lax

HEADS = 32
HD = 64
FF_A = 8192
DA = 2048
VID_DEV = 128
AUD_DEV = 2
VIDEO = 2048
AUDIO = 32


def base_field(key, shape):
    return jnp.clip(1.6 * jax.random.normal(key, shape, jnp.float32), -6.0, 6.0)


def draw_audio_qkv(key, part):
    drawn = base_field(jax.random.fold_in(key, 11), (3, AUDIO, DA))
    return drawn.astype(jnp.bfloat16)


def draw_video_qkv(key, part):
    drawn = base_field(jax.random.fold_in(key, 12), (3, VIDEO, DA))
    return drawn.astype(jnp.bfloat16)


def block_levels(stream_key, extent, shards, least, high):
    def one(dim, shards_of):
        draws = jax.random.uniform(jax.random.fold_in(jax.random.fold_in(stream_key, 6), dim), (shards_of,), jnp.float32, least / len(shards), high / len(shards))
        return jnp.repeat(jnp.exp(draws), extent[dim] // shards_of).reshape((-1,) + (1,) * (len(extent) - dim - 1))

    factor_of = one(*shards[0])
    for cut in shards[1:]:
        factor_of = factor_of * one(*cut)
    return factor_of


def bell_draw(rng, extent, scale, bound, cuts=(), kind=jnp.bfloat16):
    values = scale * jax.random.normal(rng, extent, jnp.float32)
    if cuts:
        values = values * block_levels(rng, extent, cuts, -0.22, 0.18)
    return jnp.clip(values, -bound, bound).astype(kind)


def setup_inputs(seed: int = 0, part: int = 0) -> dict:
    key_list = jax.random.split(jax.random.key(seed), 8)
    part_keys = jax.random.split(jax.random.fold_in(key_list[7], part), 8)
    return {
        "audio_stream": bell_draw(part_keys[0], (AUDIO, DA), 1.0, 6.0, ((0, 16),)),
        "audio_qkv": draw_audio_qkv(jax.random.fold_in(jax.random.fold_in(key_list[7], part), 71), part),
        "video_qkv": draw_video_qkv(jax.random.fold_in(jax.random.fold_in(key_list[7], part), 71), part),
        "attention_out": bell_draw(key_list[3], (DA, DA), DA ** -0.5, 0.125, ((0, 16),)),
        "norm_gain": jnp.clip(1.0 + 0.15 * jax.random.normal(key_list[4], (DA,), jnp.float32), 0.25, 1.75),
        "weight_in": bell_draw(key_list[5], (DA, FF_A), DA ** -0.5, 0.125, ((1, 16),)),
        "weight_out": bell_draw(key_list[6], (FF_A, DA), FF_A ** -0.5, 0.0625, ((0, 16),)),
    }


epsilon = 1e-06

def attend(queries, key_rows, value_rows):
    row_count = queries.shape[0]
    key_count = key_rows.shape[0]
    query_heads = queries.astype(jnp.float32).reshape(row_count, HEADS, HD)
    key_heads = key_rows.astype(jnp.float32).reshape(key_count, HEADS, HD)
    value_heads = value_rows.astype(jnp.float32).reshape(key_count, HEADS, HD)
    logits = jnp.einsum('rhd,shd->rhs', query_heads, key_heads) * (1.0 / math.sqrt(HD))
    highest = lax.optimization_barrier(jnp.max(logits, axis=2, keepdims=True))
    weights = jnp.exp(logits - highest)
    totals = lax.optimization_barrier(jnp.sum(weights, axis=2))
    rounded = lax.optimization_barrier(weights.astype(jnp.bfloat16))
    numerator = jnp.einsum('rhs,shd->rhd', rounded.astype(jnp.float32), value_heads)
    return (numerator / totals[:, :, None]).reshape(row_count, HEADS * HD).astype(jnp.bfloat16)

def reference(audio_stream, audio_qkv, video_qkv, attention_out, norm_gain, weight_in, weight_out):
    video_blocks = video_qkv[0].reshape(VIDEO // VID_DEV, VID_DEV, DA)
    video_mix = lax.map(lambda query_block: attend(query_block, audio_qkv[1], audio_qkv[2]), video_blocks)
    video_mix = video_mix.reshape(VIDEO, DA)
    audio_blocks = audio_qkv[0].reshape(AUDIO // AUD_DEV, AUD_DEV, DA)
    audio_attention = lax.map(lambda query_block: attend(query_block, video_qkv[1], video_qkv[2]), audio_blocks)
    audio_attention = audio_attention.reshape(AUDIO, DA)
    mixed_audio = audio_stream.astype(jnp.float32) + jnp.dot(audio_attention, attention_out, preferred_element_type=jnp.float32)
    mean_square = lax.optimization_barrier(jnp.mean(mixed_audio * mixed_audio, axis=1, keepdims=True))
    normed = (mixed_audio * lax.rsqrt(mean_square + epsilon) * norm_gain).astype(jnp.bfloat16)
    hidden = jax.nn.gelu(jnp.dot(normed, weight_in, preferred_element_type=jnp.float32), approximate=True).astype(jnp.bfloat16)
    audio_result = (mixed_audio + jnp.dot(hidden, weight_out, preferred_element_type=jnp.float32)).astype(jnp.bfloat16)
    return (video_mix, audio_result)
```

```python
import functools
import math

import jax
import jax.numpy as jnp
from jax import lax
from jax.experimental import pallas as pl
from jax.experimental.pallas import tpu as pltpu
from jax.sharding import PartitionSpec as P

HEADS = 32
HD = 64
LANES = 128
STATS = 16
EPSILON = 1e-06
SCALE = 1.0 / math.sqrt(HD)
F32 = jnp.float32
BF16 = jnp.bfloat16


def mm(a, b, ca, cb):
    return lax.dot_general(a, b, (((ca,), (cb,)), ((), ())), preferred_element_type=F32)


def lane_of(shape):
    return lax.broadcasted_iota(jnp.int32, shape, len(shape) - 1)


def kernel(
    n, stream, aqkv, vqkv, wo, gain, w1, w2,
    vmix_out, result,
    vq, vk, vv, vt, wo_v, w1_v, w2_v, vmix,
    relay, relay_own, qmat, kmat, vmat,
    g_q, g_kv, p_send, p_recv, a_send, a_recv, g_n, o_send, o_recv,
    load_sem, out_sem, send_sem, recv_sem,
):
    me = lax.axis_index("seq")
    tokens, width = stream.shape
    chunks = width // LANES
    block = tokens * chunks
    audio = n * tokens
    group = LANES // audio
    window = max(group * HD, LANES)
    windows = width // window
    subs = window // (group * HD)
    slab = wo.shape[0]
    receivers = n // (windows * subs)
    rows = HD // receivers

    def peer_of(i):
        return lax.rem(me + 1 + lax.rem(i + n // 2 - 1, n - 1), n)

    def remote(src, dst, phase, peer):
        return pltpu.make_async_remote_copy(
            src_ref=src,
            dst_ref=dst,
            send_sem=send_sem.at[phase],
            recv_sem=recv_sem.at[phase],
            device_id={"seq": peer},
            device_id_type=pl.DeviceIdType.MESH,
        )

    def each_peer(act):
        def body(i, carry):
            act(peer_of(i))
            return carry

        lax.fori_loop(0, n - 1, body, 0)

    def all_of(ref, phase):
        part = ref.at[pl.ds(0, n - 1)]
        return remote(part, part, phase, lax.rem(me + 1, n))

    barrier = pltpu.get_barrier_semaphore()
    each_peer(
        lambda peer: pl.semaphore_signal(
            barrier, inc=1, device_id={"seq": peer}, device_id_type=pl.DeviceIdType.MESH
        )
    )

    sources = (vqkv.at[1], vqkv.at[2], vqkv.at[0], wo, w1, w2)
    places = (vk, vv, vq, wo_v, w1_v, w2_v)
    loads = [
        pltpu.make_async_copy(src, dst, load_sem.at[i])
        for i, (src, dst) in enumerate(zip(sources, places))
    ]
    for load in loads:
        load.start()

    def own_blocks(value):
        for c in range(chunks):
            relay_own[pl.ds(c, tokens, stride=chunks), :] = value[:, c * LANES : (c + 1) * LANES]
        return relay_own[...]

    g_q[me] = (own_blocks(aqkv[0].astype(F32)) * SCALE).astype(BF16)
    g_kv[me, 0:block] = (own_blocks(aqkv[1].astype(F32)) * SCALE).astype(BF16)
    g_kv[me, block : 2 * block] = own_blocks(aqkv[2].astype(F32)).astype(BF16)

    pl.semaphore_wait(barrier, n - 1)
    each_peer(lambda peer: remote(g_q.at[me], g_q.at[me], 0, peer).start())
    each_peer(lambda peer: remote(g_kv.at[me], g_kv.at[me], 1, peer).start())

    def rows_of(blocks):
        relay[...] = blocks.astype(F32).reshape(audio * chunks, LANES)
        return jnp.concatenate(
            [relay[pl.ds(c, audio, stride=chunks), :].astype(BF16) for c in range(chunks)], axis=1
        )

    def blocks_of(value):
        for c in range(chunks):
            relay[pl.ds(c, audio, stride=chunks), :] = value[:, c * LANES : (c + 1) * LANES]
        return relay[...].astype(BF16).reshape(n, block, LANES)

    def diagonal(part, sub):
        head = lane_of(part.shape) // HD
        return jnp.concatenate(
            [jnp.where(head == sub * group + h, part, jnp.zeros_like(part)) for h in range(group)],
            axis=0,
        )

    loads[0].wait()
    loads[1].wait()
    for w in range(windows):
        cols = slice(w * window, (w + 1) * window)
        vt[cols, :] = vv[:, cols].T

    all_of(g_q, 0).wait_recv()
    qmat[...] = rows_of(g_q[...])

    for w in range(windows):
        cols = slice(w * window, (w + 1) * window)
        for sub in range(subs):
            scores = mm(vk[:, cols], diagonal(qmat[:, cols], sub), 1, 1)
            peak = jnp.max(scores, axis=0, keepdims=True).astype(BF16).astype(F32)
            weights = jnp.exp(scores - peak)
            total = jnp.sum(weights, axis=0, keepdims=True)
            product = mm(vt[cols, :], weights.astype(BF16), 1, 0)
            lane = lane_of((HD, LANES)) // audio
            chosen = jnp.zeros((HD, LANES), F32)
            for h in range(group):
                at = (sub * group + h) * HD
                chosen = jnp.where(lane == h, product[at : at + HD], chosen)
            high = total.astype(BF16).astype(F32)
            row = lax.broadcasted_iota(jnp.int32, (STATS, LANES), 0)
            stats = jnp.where(
                row == 0, peak, jnp.where(row == 1, high, jnp.where(row == 2, total - high, 0.0))
            )
            for j in range(receivers):
                if slab < HD:
                    numerator, mine = chosen[j * rows : (j + 1) * rows], stats
                else:
                    span = slab // HD * audio
                    numerator, mine = jnp.zeros((rows, LANES), F32), jnp.zeros((STATS, LANES), F32)
                    for i in range(LANES // span):
                        shift = (i - j) * span % LANES
                        part, part_stats = chosen[i * rows : (i + 1) * rows], stats
                        if shift:
                            part = pltpu.roll(part, shift, 1)
                            part_stats = pltpu.roll(part_stats, shift, 1)
                        numerator = jnp.where(
                            lane_of((rows, LANES)) // span == i, part, numerator
                        )
                        mine = jnp.where(lane_of((STATS, LANES)) // span == i, part_stats, mine)
                target = (w * subs + sub) * receivers + j
                p_send[target, 0:rows] = numerator.astype(BF16)
                p_send[target, rows : rows + STATS] = mine.astype(BF16)

                @pl.when(me != target)
                def _():
                    remote(p_send.at[target], p_recv.at[me], 2, target).start()

    p_recv[me] = p_send[me]

    all_of(g_kv, 1).wait_recv()
    loads[2].wait()
    kmat[...] = rows_of(g_kv[:, 0:block])
    vmat[...] = rows_of(g_kv[:, block : 2 * block])
    store = pltpu.make_async_copy(vmix, vmix_out, out_sem)

    def video(first, last):
        for w in range(first, last):
            cols = slice(w * window, (w + 1) * window)
            mixed = None
            for sub in range(subs):
                scores = mm(diagonal(kmat[:, cols], sub), vq[:, cols], 1, 1)
                scores = scores.reshape(group, audio, scores.shape[1])
                weights = jnp.exp(scores - jnp.max(scores, axis=1, keepdims=True))
                weights = weights / jnp.sum(weights, axis=1, keepdims=True)
                weights = weights.reshape(group * audio, scores.shape[2])
                term = mm(weights.T.astype(BF16), diagonal(vmat[:, cols], sub), 1, 0)
                mixed = term if mixed is None else mixed + term
            vmix[:, cols] = mixed.astype(BF16)

    video(0, windows)
    store.start()

    all_of(p_recv, 2).wait_recv()
    loads[3].wait()
    parts = p_recv[...].astype(F32)
    peaks = parts[:, rows : rows + 1]
    scales = jnp.exp(peaks - jnp.max(peaks, axis=0, keepdims=True))
    totals = (parts[:, rows + 1 : rows + 2] + parts[:, rows + 2 : rows + 3]) * scales
    attended = jnp.sum(parts[:, 0:rows] * scales, axis=0) / jnp.sum(totals, axis=0)
    turned = attended.T.astype(BF16)
    if slab < HD:
        columns = turned
    else:
        heads = slab // HD
        folds = HD // rows
        columns = jnp.concatenate(
            [
                turned[(f * heads + h) * audio : (f * heads + h + 1) * audio]
                for h in range(heads)
                for f in range(folds)
            ],
            axis=1,
        )

    def scatter(value, send, recv, phase):
        send[...] = blocks_of(value)
        each_peer(lambda peer: remote(send.at[peer], recv.at[me], phase, peer).start())
        recv[me] = send[me]

    scatter(mm(columns, wo_v[...], 1, 0), a_send, a_recv, 3)
    own = own_blocks(stream[...].astype(F32))
    all_of(a_recv, 3).wait_recv()
    mixed_audio = own + jnp.sum(a_recv[...].astype(F32), axis=0)

    by_token = mixed_audio.reshape(tokens, chunks, LANES)
    square = jnp.sum(jnp.sum(by_token * by_token, axis=1, keepdims=True), axis=2, keepdims=True)
    normed = by_token * lax.rsqrt(square / width + EPSILON) * gain[...][None]
    g_n[me] = normed.reshape(block, LANES).astype(BF16)
    each_peer(lambda peer: remote(g_n.at[me], g_n.at[me], 4, peer).start())
    loads[4].wait()
    loads[5].wait()
    all_of(g_n, 4).wait_recv()

    hidden = jax.nn.gelu(mm(rows_of(g_n[...]), w1_v[...], 1, 0), approximate=True)
    scatter(mm(hidden.astype(BF16), w2_v[...], 1, 0), o_send, o_recv, 5)
    all_of(o_recv, 5).wait_recv()
    relay_own[...] = mixed_audio + jnp.sum(o_recv[...].astype(F32), axis=0)
    for c in range(chunks):
        result[:, c * LANES : (c + 1) * LANES] = relay_own[
            pl.ds(c, tokens, stride=chunks), :
        ].astype(BF16)

    for phase, ref in enumerate((g_q, g_kv, p_send, a_send, g_n, o_send)):
        all_of(ref, phase).wait_send()
    store.wait()


def local(n, audio_stream, audio_qkv, video_qkv, attention_out, norm_gain, weight_in, weight_out):
    tokens, width = audio_stream.shape
    chunks = width // LANES
    block = tokens * chunks
    audio = n * tokens
    video = video_qkv.shape[1]
    receivers = n * LANES // (audio * HEADS)
    part = HD // receivers + STATS
    vmem = pl.BlockSpec(memory_space=pltpu.VMEM)
    anywhere = pl.BlockSpec(memory_space=pl.ANY)
    gathered = pltpu.VMEM((n, block, LANES), BF16)
    parts = pltpu.VMEM((n, part, LANES), BF16)
    return pl.pallas_call(
        functools.partial(kernel, n),
        out_shape=(
            jax.ShapeDtypeStruct((video, width), BF16),
            jax.ShapeDtypeStruct((tokens, width), BF16),
        ),
        in_specs=[vmem, vmem, anywhere, anywhere, vmem, anywhere, anywhere],
        out_specs=(anywhere, vmem),
        scratch_shapes=[
            pltpu.VMEM((video, width), BF16),
            pltpu.VMEM((video, width), BF16),
            pltpu.VMEM((video, width), BF16),
            pltpu.VMEM((width, video), BF16),
            pltpu.VMEM(attention_out.shape, BF16),
            pltpu.VMEM(weight_in.shape, BF16),
            pltpu.VMEM(weight_out.shape, BF16),
            pltpu.VMEM((video, width), BF16),
            pltpu.VMEM((audio * chunks, LANES), F32),
            pltpu.VMEM((block, LANES), F32),
            pltpu.VMEM((audio, width), BF16),
            pltpu.VMEM((audio, width), BF16),
            pltpu.VMEM((audio, width), BF16),
            gathered,
            pltpu.VMEM((n, 2 * block, LANES), BF16),
            parts,
            parts,
            gathered,
            gathered,
            gathered,
            gathered,
            gathered,
            pltpu.SemaphoreType.DMA((6,)),
            pltpu.SemaphoreType.DMA,
            pltpu.SemaphoreType.DMA((6,)),
            pltpu.SemaphoreType.DMA((6,)),
        ],
        compiler_params=pltpu.CompilerParams(
            collective_id=0, has_side_effects=True, vmem_limit_bytes=48 * 1024 * 1024
        ),
        name="cross_modal_layer",
    )(
        audio_stream,
        audio_qkv,
        video_qkv,
        attention_out,
        norm_gain.reshape(chunks, LANES),
        weight_in,
        weight_out,
    )


def solution(mesh):
    placed = (
        P(("groups", "seq"), None),
        P(None, ("groups", "seq"), None),
        P(None, ("groups", "seq"), None),
        P("seq", None),
        P(),
        P(None, "seq"),
        P("seq", None),
    )
    return jax.shard_map(
        functools.partial(local, mesh.shape["seq"]),
        mesh=mesh,
        in_specs=placed,
        out_specs=(P(("groups", "seq"), None), P(("groups", "seq"), None)),
        check_vma=False,
    )
```

```python
import functools
import math

import jax
import jax.numpy as jnp
from jax import lax
from jax.experimental import pallas as pl
from jax.experimental.pallas import tpu as pltpu
from jax.sharding import PartitionSpec as P

HEADS = 32
HD = 64
LANES = 128
STATS = 16
NEAR = 4
EPSILON = 1e-06
SCALE = 1.0 / math.sqrt(HD)
F32 = jnp.float32
BF16 = jnp.bfloat16


def mm(a, b, ca, cb):
    return lax.dot_general(a, b, (((ca,), (cb,)), ((), ())), preferred_element_type=F32)


def lane_of(shape):
    return lax.broadcasted_iota(jnp.int32, shape, len(shape) - 1)


def kernel(
    n, near, stream_in, aqkv_in, vqkv, wo, gain_in, w1, w2,
    vmix_out, result,
    stream, aqkv, gain, vq, vk, vv, vt, wo_v, w1_v, w2_v, vmix,
    relay, relay_own, qmat, kmat, vmat,
    g_q, g_kv, p_send, p_recv, a_send, a_recv, g_n, o_send, o_recv,
    load_sem, out_sem, send_sem, recv_sem,
):
    me = lax.axis_index("seq")
    tokens, width = stream.shape
    chunks = width // LANES
    block = tokens * chunks
    audio = n * tokens
    group = LANES // audio
    window = max(group * HD, LANES)
    windows = width // window
    subs = window // (group * HD)
    slab = wo.shape[0]
    receivers = n // (windows * subs)
    rows = HD // receivers

    def remote(src, dst, phase, peer):
        return pltpu.make_async_remote_copy(
            src_ref=src,
            dst_ref=dst,
            send_sem=send_sem.at[phase],
            recv_sem=recv_sem.at[phase],
            device_id={"seq": peer},
            device_id_type=pl.DeviceIdType.MESH,
        )

    def each_peer(act):
        for i in range(n - 1):
            act(lax.rem(me + 1 + (i + n // 2 - 1) % (n - 1), n))

    def all_of(ref, phase, count=n - 1):
        part = ref.at[pl.ds(0, count)]
        return remote(part, part, phase, lax.rem(me + 1, n))

    barrier = pltpu.get_barrier_semaphore()
    each_peer(
        lambda peer: pl.semaphore_signal(
            barrier, inc=1, device_id={"seq": peer}, device_id_type=pl.DeviceIdType.MESH
        )
    )

    sources = (aqkv_in, vqkv.at[1], vqkv.at[2], vqkv.at[0], wo, stream_in, gain_in, w1, w2)
    places = (aqkv, vk, vv, vq, wo_v, stream, gain, w1_v, w2_v)
    loads = [
        pltpu.make_async_copy(src, dst, load_sem.at[i])
        for i, (src, dst) in enumerate(zip(sources, places))
    ]
    for load in loads:
        load.start()

    def own_blocks(value):
        for c in range(chunks):
            relay_own[pl.ds(c, tokens, stride=chunks), :] = value[:, c * LANES : (c + 1) * LANES]
        return relay_own[...]

    far = n // near
    my_far, my_near = lax.div(me, near), lax.rem(me, near)
    kv_slot = my_near * far + my_far
    kv_row = pl.ds(my_near * far, far)

    def kv_across():
        for i in range(1, far):
            peer = lax.rem(my_far + i, far) * near + my_near
            remote(g_kv.at[kv_slot], g_kv.at[kv_slot], 1, peer).start()

    def kv_within():
        all_of(g_kv, 1, far - 1).wait_recv()
        for i in range(1, near):
            peer = my_far * near + lax.rem(my_near + i, near)
            remote(g_kv.at[kv_row], g_kv.at[kv_row], 6, peer).start()

    loads[0].wait()
    g_q[me] = (own_blocks(aqkv[0].astype(F32)) * SCALE).astype(BF16)
    g_kv[kv_slot, 0:block] = (own_blocks(aqkv[1].astype(F32)) * SCALE).astype(BF16)
    g_kv[kv_slot, block : 2 * block] = own_blocks(aqkv[2].astype(F32)).astype(BF16)

    pl.semaphore_wait(barrier, n - 1)
    each_peer(lambda peer: remote(g_q.at[me], g_q.at[me], 0, peer).start())
    kv_across()

    def rows_of(blocks):
        relay[...] = blocks.astype(F32).reshape(audio * chunks, LANES)
        return jnp.concatenate(
            [relay[pl.ds(c, audio, stride=chunks), :].astype(BF16) for c in range(chunks)], axis=1
        )

    def blocks_of(value):
        for c in range(chunks):
            relay[pl.ds(c, audio, stride=chunks), :] = value[:, c * LANES : (c + 1) * LANES]
        return relay[...].astype(BF16).reshape(n, block, LANES)

    def diagonal(part, sub):
        head = lane_of(part.shape) // HD
        return jnp.concatenate(
            [jnp.where(head == sub * group + h, part, jnp.zeros_like(part)) for h in range(group)],
            axis=0,
        )

    loads[1].wait()
    loads[2].wait()
    for w in range(windows):
        cols = slice(w * window, (w + 1) * window)
        vt[cols, :] = vv[:, cols].T

    all_of(g_q, 0).wait_recv()
    qmat[...] = rows_of(g_q[...])

    for w in range(windows):
        cols = slice(w * window, (w + 1) * window)
        for sub in range(subs):
            scores = mm(vk[:, cols], diagonal(qmat[:, cols], sub), 1, 1)
            peak = jnp.max(scores, axis=0, keepdims=True).astype(BF16).astype(F32)
            weights = jnp.exp(scores - peak)
            total = jnp.sum(weights, axis=0, keepdims=True)
            product = mm(vt[cols, :], weights.astype(BF16), 1, 0)
            lane = lane_of((HD, LANES)) // audio
            chosen = jnp.zeros((HD, LANES), F32)
            for h in range(group):
                at = (sub * group + h) * HD
                chosen = jnp.where(lane == h, product[at : at + HD], chosen)
            high = total.astype(BF16).astype(F32)
            row = lax.broadcasted_iota(jnp.int32, (STATS, LANES), 0)
            stats = jnp.where(
                row == 0, peak, jnp.where(row == 1, high, jnp.where(row == 2, total - high, 0.0))
            )
            for j in range(receivers):
                if slab < HD:
                    numerator, mine = chosen[j * rows : (j + 1) * rows], stats
                else:
                    span = slab // HD * audio
                    numerator, mine = jnp.zeros((rows, LANES), F32), jnp.zeros((STATS, LANES), F32)
                    for i in range(LANES // span):
                        shift = (i - j) * span % LANES
                        part, part_stats = chosen[i * rows : (i + 1) * rows], stats
                        if shift:
                            part = pltpu.roll(part, shift, 1)
                            part_stats = pltpu.roll(part_stats, shift, 1)
                        numerator = jnp.where(
                            lane_of((rows, LANES)) // span == i, part, numerator
                        )
                        mine = jnp.where(lane_of((STATS, LANES)) // span == i, part_stats, mine)
                target = (w * subs + sub) * receivers + j
                p_send[target, 0:rows] = numerator.astype(BF16)
                p_send[target, rows : rows + STATS] = mine.astype(BF16)

    each_peer(lambda peer: remote(p_send.at[peer], p_recv.at[me], 2, peer).start())
    kv_within()
    p_recv[me] = p_send[me]

    store = pltpu.make_async_copy(vmix, vmix_out, out_sem)

    def video(first, last):
        for w in range(first, last):
            cols = slice(w * window, (w + 1) * window)
            mixed = None
            for sub in range(subs):
                scores = mm(diagonal(kmat[:, cols], sub), vq[:, cols], 1, 1)
                scores = scores.reshape(group, audio, scores.shape[1])
                weights = jnp.exp(scores - jnp.max(scores, axis=1, keepdims=True))
                weights = weights / jnp.sum(weights, axis=1, keepdims=True)
                weights = weights.reshape(group * audio, scores.shape[2])
                term = mm(weights.T.astype(BF16), diagonal(vmat[:, cols], sub), 1, 0)
                mixed = term if mixed is None else mixed + term
            vmix[:, cols] = mixed.astype(BF16)

    all_of(p_recv, 2).wait_recv()
    loads[4].wait()
    parts = p_recv[...].astype(F32)
    peaks = parts[:, rows : rows + 1]
    scales = jnp.exp(peaks - jnp.max(peaks, axis=0, keepdims=True))
    totals = (parts[:, rows + 1 : rows + 2] + parts[:, rows + 2 : rows + 3]) * scales
    attended = jnp.sum(parts[:, 0:rows] * scales, axis=0) / jnp.sum(totals, axis=0)
    turned = attended.T.astype(BF16)
    if slab < HD:
        columns = turned
    else:
        heads = slab // HD
        folds = HD // rows
        columns = jnp.concatenate(
            [
                turned[(f * heads + h) * audio : (f * heads + h + 1) * audio]
                for h in range(heads)
                for f in range(folds)
            ],
            axis=1,
        )

    def scatter(value, send, recv, phase):
        send[...] = blocks_of(value)
        each_peer(lambda peer: remote(send.at[peer], recv.at[me], phase, peer).start())
        recv[me] = send[me]

    scatter(mm(columns, wo_v[...], 1, 0), a_send, a_recv, 3)
    loads[5].wait()
    loads[6].wait()
    own = own_blocks(stream[...].astype(F32))
    all_of(g_kv, 6, far * (near - 1)).wait_recv()
    loads[3].wait()
    kmat[...] = rows_of(g_kv[:, 0:block])
    vmat[...] = rows_of(g_kv[:, block : 2 * block])
    video(0, windows // 2)
    all_of(a_recv, 3).wait_recv()
    mixed_audio = own + jnp.sum(a_recv[...].astype(F32), axis=0)

    by_token = mixed_audio.reshape(tokens, chunks, LANES)
    square = jnp.sum(jnp.sum(by_token * by_token, axis=1, keepdims=True), axis=2, keepdims=True)
    normed = by_token * lax.rsqrt(square / width + EPSILON) * gain[...][None]
    g_n[me] = normed.reshape(block, LANES).astype(BF16)
    each_peer(lambda peer: remote(g_n.at[me], g_n.at[me], 4, peer).start())
    video(windows // 2, windows)
    store.start()
    loads[7].wait()
    loads[8].wait()
    all_of(g_n, 4).wait_recv()

    hidden = jax.nn.gelu(mm(rows_of(g_n[...]), w1_v[...], 1, 0), approximate=True)
    scatter(mm(hidden.astype(BF16), w2_v[...], 1, 0), o_send, o_recv, 5)
    all_of(o_recv, 5).wait_recv()
    relay_own[...] = mixed_audio + jnp.sum(o_recv[...].astype(F32), axis=0)
    for c in range(chunks):
        result[:, c * LANES : (c + 1) * LANES] = relay_own[
            pl.ds(c, tokens, stride=chunks), :
        ].astype(BF16)

    all_of(g_kv, 1, far - 1).wait_send()
    all_of(g_kv, 6, far * (near - 1)).wait_send()
    for phase, ref in ((0, g_q), (2, p_send), (3, a_send), (4, g_n), (5, o_send)):
        all_of(ref, phase).wait_send()
    store.wait()


def local(n, audio_stream, audio_qkv, video_qkv, attention_out, norm_gain, weight_in, weight_out):
    tokens, width = audio_stream.shape
    chunks = width // LANES
    block = tokens * chunks
    audio = n * tokens
    video = video_qkv.shape[1]
    receivers = n * LANES // (audio * HEADS)
    part = HD // receivers + STATS
    vmem = pl.BlockSpec(memory_space=pltpu.VMEM)
    anywhere = pl.BlockSpec(memory_space=pltpu.HBM)
    gathered = pltpu.VMEM((n, block, LANES), BF16)
    parts = pltpu.VMEM((n, part, LANES), BF16)
    return pl.pallas_call(
        functools.partial(kernel, n, math.gcd(n, NEAR)),
        out_shape=(
            jax.ShapeDtypeStruct((video, width), BF16),
            jax.ShapeDtypeStruct((tokens, width), BF16),
        ),
        in_specs=[anywhere] * 7,
        out_specs=(anywhere, vmem),
        scratch_shapes=[
            pltpu.VMEM(audio_stream.shape, BF16),
            pltpu.VMEM(audio_qkv.shape, BF16),
            pltpu.VMEM((chunks, LANES), F32),
            pltpu.VMEM((video, width), BF16),
            pltpu.VMEM((video, width), BF16),
            pltpu.VMEM((video, width), BF16),
            pltpu.VMEM((width, video), BF16),
            pltpu.VMEM(attention_out.shape, BF16),
            pltpu.VMEM(weight_in.shape, BF16),
            pltpu.VMEM(weight_out.shape, BF16),
            pltpu.VMEM((video, width), BF16),
            pltpu.VMEM((audio * chunks, LANES), F32),
            pltpu.VMEM((block, LANES), F32),
            pltpu.VMEM((audio, width), BF16),
            pltpu.VMEM((audio, width), BF16),
            pltpu.VMEM((audio, width), BF16),
            gathered,
            pltpu.VMEM((n, 2 * block, LANES), BF16),
            parts,
            parts,
            gathered,
            gathered,
            gathered,
            gathered,
            gathered,
            pltpu.SemaphoreType.DMA((9,)),
            pltpu.SemaphoreType.DMA,
            pltpu.SemaphoreType.DMA((7,)),
            pltpu.SemaphoreType.DMA((7,)),
        ],
        compiler_params=pltpu.CompilerParams(
            collective_id=0, has_side_effects=True, vmem_limit_bytes=60 * 1024 * 1024
        ),
        name="cross_modal_layer",
    )(
        audio_stream,
        audio_qkv,
        video_qkv,
        attention_out,
        norm_gain.reshape(chunks, LANES),
        weight_in,
        weight_out,
    )


def solution(mesh):
    placed = (
        P(("groups", "seq"), None),
        P(None, ("groups", "seq"), None),
        P(None, ("groups", "seq"), None),
        P("seq", None),
        P(),
        P(None, "seq"),
        P("seq", None),
    )
    return jax.shard_map(
        functools.partial(local, mesh.shape["seq"]),
        mesh=mesh,
        in_specs=placed,
        out_specs=(P(("groups", "seq"), None), P(("groups", "seq"), None)),
        check_vma=False,
    )
```

```python
import functools
import math

import jax
import jax.numpy as jnp
from jax import lax
from jax.experimental import pallas as pl
from jax.experimental.pallas import tpu as pltpu
from jax.sharding import PartitionSpec as P

HEADS = 32
HD = 64
LANES = 128
STATS = 16
NEAR = 4
PIECES = 4
EPSILON = 1e-06
SCALE = 1.0 / math.sqrt(HD)
F32 = jnp.float32
BF16 = jnp.bfloat16


def mm(a, b, ca, cb):
    return lax.dot_general(a, b, (((ca,), (cb,)), ((), ())), preferred_element_type=F32)


def lane_of(shape):
    return lax.broadcasted_iota(jnp.int32, shape, len(shape) - 1)


def kernel(
    n, near, stream_in, aqkv_in, vqkv, wo, gain_in, w1, w2,
    vmix_out, result,
    stream, aqkv, gain, vq, vk, vv, vt, wo_v, w1_v, w2_v, vmix,
    relay, relay_own, qmat, kmat, vmat,
    q_send, g_q, g_kv, p_send, p_recv, a_send, a_recv, g_n, o_send, o_recv,
    load_sem, out_sem, send_sem, recv_sem,
):
    me = lax.axis_index("seq")
    tokens, width = stream.shape
    chunks = width // LANES
    block = tokens * chunks
    audio = n * tokens
    group = LANES // audio
    window = max(group * HD, LANES)
    windows = width // window
    subs = window // (group * HD)
    slab = wo.shape[0]
    receivers = n // (windows * subs)
    rows = HD // receivers

    def remote(src, dst, phase, peer):
        return pltpu.make_async_remote_copy(
            src_ref=src,
            dst_ref=dst,
            send_sem=send_sem.at[phase],
            recv_sem=recv_sem.at[phase],
            device_id={"seq": peer},
            device_id_type=pl.DeviceIdType.MESH,
        )

    def each_peer(act):
        for i in range(n - 1):
            act(lax.rem(me + 1 + (i + n // 2 - 1) % (n - 1), n))

    def all_of(ref, phase, count=n - 1):
        part = ref.at[pl.ds(0, count)]
        return remote(part, part, phase, lax.rem(me + 1, n))

    barrier = pltpu.get_barrier_semaphore()
    each_peer(
        lambda peer: pl.semaphore_signal(
            barrier, inc=1, device_id={"seq": peer}, device_id_type=pl.DeviceIdType.MESH
        )
    )

    core = lax.rem(me, 2)
    chip = lax.div(me, 2)
    partner = me + 1 - 2 * core
    half = n // 2
    wide = width // 2
    mine = pl.ds(pl.multiple_of(core * wide, LANES), wide)
    theirs = pl.ds(pl.multiple_of((1 - core) * wide, LANES), wide)
    keys = vqkv.shape[1]
    first, second = pl.ds(0, keys), pl.ds(keys, keys)

    sources = (aqkv_in, vqkv.at[1, :, mine], vqkv.at[2, :, mine], vqkv.at[0], wo, stream_in, gain_in, w1, w2)
    places = (aqkv, vk.at[first], vv.at[first], vq, wo_v, stream, gain, w1_v, w2_v)
    loads = [
        pltpu.make_async_copy(src, dst, load_sem.at[i])
        for i, (src, dst) in enumerate(zip(sources, places))
    ]
    for load in loads:
        load.start()

    def own_blocks(value):
        for c in range(chunks):
            relay_own[pl.ds(c, tokens, stride=chunks), :] = value[:, c * LANES : (c + 1) * LANES]
        return relay_own[...]

    far = n // near
    my_far, my_near = lax.div(me, near), lax.rem(me, near)
    kv_slot = my_near * far + my_far
    kv_row = pl.ds(my_near * far, far)

    def kv_across():
        for i in range(1, far):
            peer = lax.rem(my_far + i, far) * near + my_near
            remote(g_kv.at[kv_slot], g_kv.at[kv_slot], 1, peer).start()

    def kv_within():
        all_of(g_kv, 1, far - 1).wait_recv()
        for i in range(1, near):
            peer = my_far * near + lax.rem(my_near + i, near)
            remote(g_kv.at[kv_row], g_kv.at[kv_row], 6, peer).start()

    loads[0].wait()
    queries = (own_blocks(aqkv[0].astype(F32)) * SCALE).reshape(tokens, 2, chunks // 2, LANES)
    for h in range(2):
        q_send[h] = queries[:, h].reshape(block // 2, LANES).astype(BF16)
    g_q[me] = q_send[core]
    g_kv[kv_slot, 0:block] = (own_blocks(aqkv[1].astype(F32)) * SCALE).astype(BF16)
    g_kv[kv_slot, block : 2 * block] = own_blocks(aqkv[2].astype(F32)).astype(BF16)

    pl.semaphore_wait(barrier, n - 1)
    shared = [
        remote(vqkv.at[1 + i, :, theirs], ref.at[second], 7 + i, partner)
        for i, ref in enumerate((vk, vv))
    ]
    for copy in shared:
        copy.start()
    each_peer(lambda peer: remote(q_send.at[lax.rem(peer, 2)], g_q.at[me], 0, peer).start())
    kv_across()

    def rows_of(blocks):
        count = blocks.shape[0] * blocks.shape[1]
        step = count // audio
        relay[0:count] = blocks.astype(F32).reshape(count, LANES)
        return jnp.concatenate(
            [relay[pl.ds(c, audio, stride=step), :].astype(BF16) for c in range(step)], axis=1
        )

    def blocks_of(value):
        for c in range(chunks):
            relay[pl.ds(c, audio, stride=chunks), :] = value[:, c * LANES : (c + 1) * LANES]
        return relay[...].astype(BF16).reshape(n, block, LANES)

    def diagonal(part, sub):
        head = lane_of(part.shape) // HD
        return jnp.concatenate(
            [jnp.where(head == sub * group + h, part, jnp.zeros_like(part)) for h in range(group)],
            axis=0,
        )

    loads[1].wait()
    loads[2].wait()
    for copy in shared:
        copy.wait_recv()
    for w in range(windows // 2):
        cols = slice(w * window, (w + 1) * window)
        vt[cols, :] = vv[:, cols].T

    all_of(g_q, 0).wait_recv()
    qmat[...] = rows_of(g_q[...])

    for w in range(windows // 2):
        cols = slice(w * window, (w + 1) * window)
        for sub in range(subs):
            scores = mm(vk[:, cols], diagonal(qmat[:, cols], sub), 1, 1)
            peak = jnp.max(scores, axis=0, keepdims=True).astype(BF16).astype(F32)
            weights = jnp.exp(scores - peak)
            total = jnp.sum(weights, axis=0, keepdims=True)
            product = mm(vt[cols, :], weights.astype(BF16), 1, 0)
            lane = lane_of((HD, LANES)) // audio
            chosen = jnp.zeros((HD, LANES), F32)
            for h in range(group):
                at = (sub * group + h) * HD
                chosen = jnp.where(lane == h, product[at : at + HD], chosen)
            high = total.astype(BF16).astype(F32)
            row = lax.broadcasted_iota(jnp.int32, (STATS, LANES), 0)
            stats = jnp.where(
                row == 0, peak, jnp.where(row == 1, high, jnp.where(row == 2, total - high, 0.0))
            )
            for j in range(receivers):
                if slab < HD:
                    numerator, kept = chosen[j * rows : (j + 1) * rows], stats
                else:
                    span = slab // HD * audio
                    numerator, kept = jnp.zeros((rows, LANES), F32), jnp.zeros((STATS, LANES), F32)
                    for i in range(LANES // span):
                        shift = (i - j) * span % LANES
                        part, part_stats = chosen[i * rows : (i + 1) * rows], stats
                        if shift:
                            part = pltpu.roll(part, shift, 1)
                            part_stats = pltpu.roll(part_stats, shift, 1)
                        numerator = jnp.where(
                            lane_of((rows, LANES)) // span == i, part, numerator
                        )
                        kept = jnp.where(lane_of((STATS, LANES)) // span == i, part_stats, kept)
                target = (w * subs + sub) * receivers + j
                p_send[target, 0:rows] = numerator.astype(BF16)
                p_send[target, rows : rows + STATS] = kept.astype(BF16)

    for i in range(half):
        index = lax.rem(chip + (i + half // 2) % half, half)
        target = core * half + index

        @pl.when(me != target)
        def _():
            remote(p_send.at[index], p_recv.at[chip], 2, target).start()

    kv_within()
    own_part = lax.div(me, half) == core

    @pl.when(own_part)
    def _():
        p_recv[chip] = p_send[me - core * half]

    store = pltpu.make_async_copy(vmix, vmix_out, out_sem)

    def video(first, last):
        for w in range(first, last):
            cols = slice(w * window, (w + 1) * window)
            mixed = None
            for sub in range(subs):
                scores = mm(diagonal(kmat[:, cols], sub), vq[:, cols], 1, 1)
                scores = scores.reshape(group, audio, scores.shape[1])
                weights = jnp.exp(scores - jnp.max(scores, axis=1, keepdims=True))
                weights = weights / jnp.sum(weights, axis=1, keepdims=True)
                weights = weights.reshape(group * audio, scores.shape[2])
                term = mm(weights.T.astype(BF16), diagonal(vmat[:, cols], sub), 1, 0)
                mixed = term if mixed is None else mixed + term
            vmix[:, cols] = mixed.astype(BF16)

    @pl.when(own_part)
    def _():
        all_of(p_recv, 2, half - 1).wait_recv()

    @pl.when(jnp.logical_not(own_part))
    def _():
        all_of(p_recv, 2, half).wait_recv()

    loads[4].wait()
    parts = p_recv[...].astype(F32)
    peaks = parts[:, rows : rows + 1]
    scales = jnp.exp(peaks - jnp.max(peaks, axis=0, keepdims=True))
    totals = (parts[:, rows + 1 : rows + 2] + parts[:, rows + 2 : rows + 3]) * scales
    attended = jnp.sum(parts[:, 0:rows] * scales, axis=0) / jnp.sum(totals, axis=0)
    turned = attended.T.astype(BF16)
    if slab < HD:
        columns = turned
    else:
        heads = slab // HD
        folds = HD // rows
        columns = jnp.concatenate(
            [
                turned[(f * heads + h) * audio : (f * heads + h + 1) * audio]
                for h in range(heads)
                for f in range(folds)
            ],
            axis=1,
        )

    def scatter(value, send, recv, phase):
        send[...] = blocks_of(value)
        each_peer(lambda peer: remote(send.at[peer], recv.at[me], phase, peer).start())
        recv[me] = send[me]

    scatter(mm(columns, wo_v[...], 1, 0), a_send, a_recv, 3)
    loads[5].wait()
    loads[6].wait()
    own = own_blocks(stream[...].astype(F32))
    all_of(g_kv, 6, far * (near - 1)).wait_recv()
    loads[3].wait()
    kmat[...] = rows_of(g_kv[:, 0:block])
    vmat[...] = rows_of(g_kv[:, block : 2 * block])
    video(0, windows // 2)
    all_of(a_recv, 3).wait_recv()
    mixed_audio = own + jnp.sum(a_recv[...].astype(F32), axis=0)

    by_token = mixed_audio.reshape(tokens, chunks, LANES)
    square = jnp.sum(jnp.sum(by_token * by_token, axis=1, keepdims=True), axis=2, keepdims=True)
    normed = by_token * lax.rsqrt(square / width + EPSILON) * gain[...][None]
    g_n[me] = normed.reshape(block, LANES).astype(BF16)
    each_peer(lambda peer: remote(g_n.at[me], g_n.at[me], 4, peer).start())
    video(windows // 2, windows)
    store.start()
    loads[7].wait()
    loads[8].wait()
    all_of(g_n, 4).wait_recv()

    hidden = jax.nn.gelu(mm(rows_of(g_n[...]), w1_v[...], 1, 0), approximate=True)
    scatter(mm(hidden.astype(BF16), w2_v[...], 1, 0), o_send, o_recv, 5)
    all_of(o_recv, 5).wait_recv()
    relay_own[...] = mixed_audio + jnp.sum(o_recv[...].astype(F32), axis=0)
    for c in range(chunks):
        result[:, c * LANES : (c + 1) * LANES] = relay_own[
            pl.ds(c, tokens, stride=chunks), :
        ].astype(BF16)

    all_of(g_kv, 1, far - 1).wait_send()
    all_of(g_kv, 6, far * (near - 1)).wait_send()
    for copy in shared:
        copy.wait_send()

    @pl.when(own_part)
    def _():
        all_of(p_send, 2, half - 1).wait_send()

    @pl.when(jnp.logical_not(own_part))
    def _():
        all_of(p_send, 2, half).wait_send()

    for phase, ref in ((0, g_q), (3, a_send), (4, g_n), (5, o_send)):
        all_of(ref, phase).wait_send()
    store.wait()


def write_results(mixed, result, mixed_out, result_out, sem):
    size = mixed.shape[0] // PIECES
    copies = [pltpu.make_async_copy(result, result_out, sem.at[PIECES])]
    for i in range(PIECES):
        rows = pl.ds(i * size, size)
        copies.append(pltpu.make_async_copy(mixed.at[rows], mixed_out.at[rows], sem.at[i]))
    for copy in copies:
        copy.start()
    for copy in copies:
        copy.wait()


def local(n, audio_stream, audio_qkv, video_qkv, attention_out, norm_gain, weight_in, weight_out):
    tokens, width = audio_stream.shape
    chunks = width // LANES
    block = tokens * chunks
    audio = n * tokens
    video = video_qkv.shape[1]
    receivers = n * LANES // (audio * HEADS)
    part = HD // receivers + STATS
    vmem = pl.BlockSpec(memory_space=pltpu.VMEM)
    anywhere = pl.BlockSpec(memory_space=pltpu.HBM)
    gathered = pltpu.VMEM((n, block, LANES), BF16)
    parts = pltpu.VMEM((n // 2, part, LANES), BF16)
    mixed, result = pl.pallas_call(
        functools.partial(kernel, n, math.gcd(n, NEAR)),
        out_shape=(
            jax.ShapeDtypeStruct((video, width), BF16),
            jax.ShapeDtypeStruct((tokens, width), BF16),
        ),
        in_specs=[anywhere] * 7,
        out_specs=(anywhere, vmem),
        scratch_shapes=[
            pltpu.VMEM(audio_stream.shape, BF16),
            pltpu.VMEM(audio_qkv.shape, BF16),
            pltpu.VMEM((chunks, LANES), F32),
            pltpu.VMEM((video, width), BF16),
            pltpu.VMEM((2 * video, width // 2), BF16),
            pltpu.VMEM((2 * video, width // 2), BF16),
            pltpu.VMEM((width // 2, 2 * video), BF16),
            pltpu.VMEM(attention_out.shape, BF16),
            pltpu.VMEM(weight_in.shape, BF16),
            pltpu.VMEM(weight_out.shape, BF16),
            pltpu.VMEM((video, width), BF16),
            pltpu.VMEM((audio * chunks, LANES), F32),
            pltpu.VMEM((block, LANES), F32),
            pltpu.VMEM((audio, width // 2), BF16),
            pltpu.VMEM((audio, width), BF16),
            pltpu.VMEM((audio, width), BF16),
            pltpu.VMEM((2, block // 2, LANES), BF16),
            pltpu.VMEM((n, block // 2, LANES), BF16),
            pltpu.VMEM((n, 2 * block, LANES), BF16),
            parts,
            parts,
            gathered,
            gathered,
            gathered,
            gathered,
            gathered,
            pltpu.SemaphoreType.DMA((9,)),
            pltpu.SemaphoreType.DMA,
            pltpu.SemaphoreType.DMA((9,)),
            pltpu.SemaphoreType.DMA((9,)),
        ],
        compiler_params=pltpu.CompilerParams(
            collective_id=0, has_side_effects=True, vmem_limit_bytes=60 * 1024 * 1024
        ),
        name="cross_modal_layer",
    )(
        audio_stream,
        audio_qkv,
        video_qkv,
        attention_out,
        norm_gain.reshape(chunks, LANES),
        weight_in,
        weight_out,
    )
    return pl.pallas_call(
        write_results,
        out_shape=(
            jax.ShapeDtypeStruct(mixed.shape, BF16),
            jax.ShapeDtypeStruct(result.shape, BF16),
        ),
        in_specs=[anywhere] * 2,
        out_specs=(anywhere, anywhere),
        scratch_shapes=[pltpu.SemaphoreType.DMA((PIECES + 1,))],
        compiler_params=pltpu.CompilerParams(vmem_limit_bytes=60 * 1024 * 1024),
        name="write_results",
    )(mixed, result)


def solution(mesh):
    placed = (
        P(("groups", "seq"), None),
        P(None, ("groups", "seq"), None),
        P(None, ("groups", "seq"), None),
        P("seq", None),
        P(),
        P(None, "seq"),
        P("seq", None),
    )
    return jax.shard_map(
        functools.partial(local, mesh.shape["seq"]),
        mesh=mesh,
        in_specs=placed,
        out_specs=(P(("groups", "seq"), None), P(("groups", "seq"), None)),
        check_vma=False,
    )
```

```python
import functools
import math

import jax
import jax.numpy as jnp
from jax import lax
from jax.experimental import pallas as pl
from jax.experimental.pallas import tpu as pltpu
from jax.sharding import PartitionSpec as P

HEADS = 32
HD = 64
LANES = 128
STATS = 16
NEAR = 4
PIECES = 4
EPSILON = 1e-06
SCALE = 1.0 / math.sqrt(HD)
F32 = jnp.float32
BF16 = jnp.bfloat16


def mm(a, b, ca, cb):
    return lax.dot_general(a, b, (((ca,), (cb,)), ((), ())), preferred_element_type=F32)


def lane_of(shape):
    return lax.broadcasted_iota(jnp.int32, shape, len(shape) - 1)


def kernel(
    n, near, stream_in, aqkv_in, vqkv, wo, gain_in, w1, w2,
    vmix_out, result,
    stream, aqkv, gain, vq, vk, vv, vt, wo_v, w1_v, w2_v, vmix,
    relay, relay_own, qmat, kmat, vmat,
    attended_v, x_send, x_recv, n_send,
    q_send, g_q, g_kv, p_send, p_recv, a_send, a_recv, g_n, o_send, o_recv,
    load_sem, out_sem, send_sem, recv_sem,
):
    me = lax.axis_index("seq")
    tokens, width = stream.shape
    chunks = width // LANES
    block = tokens * chunks
    audio = n * tokens
    group = LANES // audio
    window = max(group * HD, LANES)
    windows = width // window
    subs = window // (group * HD)
    slab = wo.shape[0]
    receivers = n // (windows * subs)
    rows = HD // receivers

    def remote(src, dst, phase, peer):
        return pltpu.make_async_remote_copy(
            src_ref=src,
            dst_ref=dst,
            send_sem=send_sem.at[phase],
            recv_sem=recv_sem.at[phase],
            device_id={"seq": peer},
            device_id_type=pl.DeviceIdType.MESH,
        )

    def each_peer(act):
        for i in range(n - 1):
            act(lax.rem(me + 1 + (i + n // 2 - 1) % (n - 1), n))

    def all_of(ref, phase, count=n - 1):
        part = ref.at[pl.ds(0, count)]
        return remote(part, part, phase, lax.rem(me + 1, n))

    barrier = pltpu.get_barrier_semaphore()
    each_peer(
        lambda peer: pl.semaphore_signal(
            barrier, inc=1, device_id={"seq": peer}, device_id_type=pl.DeviceIdType.MESH
        )
    )

    core = lax.rem(me, 2)
    chip = lax.div(me, 2)
    partner = me + 1 - 2 * core
    half = n // 2
    wide = width // 2
    mine = pl.ds(pl.multiple_of(core * wide, LANES), wide)
    theirs = pl.ds(pl.multiple_of((1 - core) * wide, LANES), wide)
    keys = vqkv.shape[1]
    first, second = pl.ds(0, keys), pl.ds(keys, keys)

    sources = (
        aqkv_in, vqkv.at[1, :, mine], vqkv.at[2, :, mine], vqkv.at[0], wo.at[:, mine],
        stream_in, gain_in, w1.at[mine], w2.at[:, mine],
    )
    places = (
        aqkv, vk.at[first], vv.at[first], vq, wo_v.at[core],
        stream, gain, w1_v.at[core], w2_v.at[core],
    )
    loads = [
        pltpu.make_async_copy(src, dst, load_sem.at[i])
        for i, (src, dst) in enumerate(zip(sources, places))
    ]
    for load in loads:
        load.start()

    def own_rows(c, split):
        step = chunks // split
        return pl.ds(c // step * tokens * step + c % step, tokens, stride=step)

    def own_blocks(value, split=1):
        for c in range(chunks):
            relay_own[own_rows(c, split), :] = value[:, c * LANES : (c + 1) * LANES]
        return relay_own[...]

    far = n // near
    my_far, my_near = lax.div(me, near), lax.rem(me, near)
    kv_slot = my_near * far + my_far
    kv_row = pl.ds(my_near * far, far)

    def kv_across():
        for i in range(1, far):
            peer = lax.rem(my_far + i, far) * near + my_near
            remote(g_kv.at[kv_slot], g_kv.at[kv_slot], 1, peer).start()

    def kv_within():
        all_of(g_kv, 1, far - 1).wait_recv()
        for i in range(1, near):
            peer = my_far * near + lax.rem(my_near + i, near)
            remote(g_kv.at[kv_row], g_kv.at[kv_row], 6, peer).start()

    loads[0].wait()
    queries = own_blocks(aqkv[0].astype(F32), 2) * SCALE
    q_send[...] = queries.astype(BF16).reshape(q_send.shape)
    g_q[me] = q_send[core]
    g_kv[kv_slot, 0:block] = (own_blocks(aqkv[1].astype(F32)) * SCALE).astype(BF16)
    g_kv[kv_slot, block : 2 * block] = own_blocks(aqkv[2].astype(F32)).astype(BF16)

    pl.semaphore_wait(barrier, n - 1)
    shared = [
        remote(vqkv.at[1 + i, :, theirs], ref.at[second], 7 + i, partner)
        for i, ref in enumerate((vk, vv))
    ]
    for copy in shared:
        copy.start()
    each_peer(lambda peer: remote(q_send.at[lax.rem(peer, 2)], g_q.at[me], 0, peer).start())
    kv_across()

    def rows_of(blocks):
        count = blocks.shape[0] * blocks.shape[1]
        step = count // audio
        relay[0:count] = blocks.astype(F32).reshape(count, LANES)
        return jnp.concatenate(
            [relay[pl.ds(c, audio, stride=step), :].astype(BF16) for c in range(step)], axis=1
        )

    def blocks_of(value):
        step = chunks // 2
        for c in range(step):
            relay[pl.ds(c, audio, stride=step), :] = value[:, c * LANES : (c + 1) * LANES]
        return relay[0 : audio * step].astype(BF16).reshape(n, block // 2, LANES)

    def diagonal(part, sub):
        head = lane_of(part.shape) // HD
        return jnp.concatenate(
            [jnp.where(head == sub * group + h, part, jnp.zeros_like(part)) for h in range(group)],
            axis=0,
        )

    loads[1].wait()
    loads[2].wait()
    for copy in shared:
        copy.wait_recv()
    for w in range(windows // 2):
        cols = slice(w * window, (w + 1) * window)
        vt[cols, :] = vv[:, cols].T

    all_of(g_q, 0).wait_recv()
    qmat[...] = rows_of(g_q[...])

    for w in range(windows // 2):
        cols = slice(w * window, (w + 1) * window)
        for sub in range(subs):
            scores = mm(vk[:, cols], diagonal(qmat[:, cols], sub), 1, 1)
            peak = jnp.max(scores, axis=0, keepdims=True).astype(BF16).astype(F32)
            weights = jnp.exp(scores - peak)
            total = jnp.sum(weights, axis=0, keepdims=True)
            product = mm(vt[cols, :], weights.astype(BF16), 1, 0)
            lane = lane_of((HD, LANES)) // audio
            chosen = jnp.zeros((HD, LANES), F32)
            for h in range(group):
                at = (sub * group + h) * HD
                chosen = jnp.where(lane == h, product[at : at + HD], chosen)
            high = total.astype(BF16).astype(F32)
            row = lax.broadcasted_iota(jnp.int32, (STATS, LANES), 0)
            stats = jnp.where(
                row == 0, peak, jnp.where(row == 1, high, jnp.where(row == 2, total - high, 0.0))
            )
            for j in range(receivers):
                if slab < HD:
                    numerator, kept = chosen[j * rows : (j + 1) * rows], stats
                else:
                    span = slab // HD * audio
                    numerator, kept = jnp.zeros((rows, LANES), F32), jnp.zeros((STATS, LANES), F32)
                    for i in range(LANES // span):
                        shift = (i - j) * span % LANES
                        part, part_stats = chosen[i * rows : (i + 1) * rows], stats
                        if shift:
                            part = pltpu.roll(part, shift, 1)
                            part_stats = pltpu.roll(part_stats, shift, 1)
                        numerator = jnp.where(
                            lane_of((rows, LANES)) // span == i, part, numerator
                        )
                        kept = jnp.where(lane_of((STATS, LANES)) // span == i, part_stats, kept)
                target = (w * subs + sub) * receivers + j
                p_send[target, 0:rows] = numerator.astype(BF16)
                p_send[target, rows : rows + STATS] = kept.astype(BF16)

    for i in range(half):
        index = lax.rem(chip + (i + half // 2) % half, half)
        target = core * half + index

        @pl.when(me != target)
        def _():
            remote(p_send.at[index], p_recv.at[chip], 2, target).start()

    kv_within()
    weights_shared = [
        remote(wo.at[:, theirs], wo_v.at[core], 9, partner),
        remote(w1.at[theirs], w1_v.at[core], 10, partner),
        remote(w2.at[:, theirs], w2_v.at[core], 11, partner),
    ]
    for copy in weights_shared:
        copy.start()
    own_part = lax.div(me, half) == core

    @pl.when(own_part)
    def _():
        p_recv[chip] = p_send[me - core * half]

    store = pltpu.make_async_copy(vmix, vmix_out, out_sem)

    def video(first, last):
        for w in range(first, last):
            cols = slice(w * window, (w + 1) * window)
            mixed = None
            for sub in range(subs):
                scores = mm(diagonal(kmat[:, cols], sub), vq[:, cols], 1, 1)
                scores = scores.reshape(group, audio, scores.shape[1])
                weights = jnp.exp(scores - jnp.max(scores, axis=1, keepdims=True))
                weights = weights / jnp.sum(weights, axis=1, keepdims=True)
                weights = weights.reshape(group * audio, scores.shape[2])
                term = mm(weights.T.astype(BF16), diagonal(vmat[:, cols], sub), 1, 0)
                mixed = term if mixed is None else mixed + term
            vmix[:, cols] = mixed.astype(BF16)

    @pl.when(own_part)
    def _():
        all_of(p_recv, 2, half - 1).wait_recv()

    @pl.when(jnp.logical_not(own_part))
    def _():
        all_of(p_recv, 2, half).wait_recv()

    parts = p_recv[...].astype(F32)
    peaks = parts[:, rows : rows + 1]
    scales = jnp.exp(peaks - jnp.max(peaks, axis=0, keepdims=True))
    totals = (parts[:, rows + 1 : rows + 2] + parts[:, rows + 2 : rows + 3]) * scales
    attended = jnp.sum(parts[:, 0:rows] * scales, axis=0) / jnp.sum(totals, axis=0)
    turned = attended.T.astype(BF16)
    if slab < HD:
        columns = turned
    else:
        heads = slab // HD
        folds = HD // rows
        columns = jnp.concatenate(
            [
                turned[(f * heads + h) * audio : (f * heads + h + 1) * audio]
                for h in range(heads)
                for f in range(folds)
            ],
            axis=1,
        )

    def scatter(value, send, recv, phase):
        send[...] = blocks_of(value)
        each_peer(lambda peer: remote(send.at[peer], recv.at[me], phase, peer).start())
        recv[me] = send[me]

    def gathered_sum(recv):
        total = jnp.sum(recv[...].astype(F32).reshape(half, block, LANES), axis=0)
        return total.reshape(2, tokens, chunks // 2, LANES)

    attended_v[core] = columns
    swap = remote(attended_v.at[core], attended_v.at[core], 12, partner)
    swap.start()
    loads[4].wait()
    part = mm(columns, wo_v[core], 1, 0)
    weights_shared[0].wait_recv()
    swap.wait_recv()
    part = part + mm(attended_v[1 - core], wo_v[1 - core], 1, 0)
    scatter(part, a_send, a_recv, 3)
    loads[5].wait()
    loads[6].wait()
    own = own_blocks(stream[...].astype(F32), 2).reshape(2, tokens, chunks // 2, LANES)
    all_of(g_kv, 6, far * (near - 1)).wait_recv()
    loads[3].wait()
    kmat[...] = rows_of(g_kv[:, 0:block])
    vmat[...] = rows_of(g_kv[:, block : 2 * block])
    video(0, windows // 2)
    all_of(a_recv, 3).wait_recv()
    mixed_audio = own + gathered_sum(a_recv)

    square = jnp.sum(mixed_audio * mixed_audio, axis=2, keepdims=True)
    square = jnp.sum(jnp.sum(square, axis=0, keepdims=True), axis=3, keepdims=True)
    scaled = gain[...].reshape(2, 1, chunks // 2, LANES)
    normed = mixed_audio * lax.rsqrt(square / width + EPSILON) * scaled
    n_send[...] = normed.reshape(2, block // 2, LANES).astype(BF16)
    g_n[me] = n_send[core]
    each_peer(lambda peer: remote(n_send.at[lax.rem(peer, 2)], g_n.at[me], 4, peer).start())
    video(windows // 2, windows)
    store.start()
    loads[7].wait()
    loads[8].wait()
    weights_shared[1].wait_recv()
    weights_shared[2].wait_recv()
    all_of(g_n, 4).wait_recv()

    features = rows_of(g_n[...])
    for k in range(2):
        x_send[k] = mm(features, w1_v[k], 1, 0)
    trade = remote(x_send, x_recv, 13, partner)
    trade.start()
    trade.wait_recv()
    part = None
    for k in range(2):
        hidden = jax.nn.gelu(x_send[k] + x_recv[k], approximate=True).astype(BF16)
        term = mm(hidden, w2_v[k], 1, 0)
        part = term if part is None else part + term
    scatter(part, o_send, o_recv, 5)
    all_of(o_recv, 5).wait_recv()
    relay_own[...] = (mixed_audio + gathered_sum(o_recv)).reshape(block, LANES)
    for c in range(chunks):
        result[:, c * LANES : (c + 1) * LANES] = relay_own[own_rows(c, 2), :].astype(BF16)

    for copy in weights_shared + [swap, trade]:
        copy.wait_send()
    all_of(g_kv, 1, far - 1).wait_send()
    all_of(g_kv, 6, far * (near - 1)).wait_send()
    for copy in shared:
        copy.wait_send()

    @pl.when(own_part)
    def _():
        all_of(p_send, 2, half - 1).wait_send()

    @pl.when(jnp.logical_not(own_part))
    def _():
        all_of(p_send, 2, half).wait_send()

    for phase, ref in ((0, g_q), (3, a_send), (4, g_n), (5, o_send)):
        all_of(ref, phase).wait_send()
    store.wait()


def write_results(mixed, result, mixed_out, result_out, mixed_v, result_v, sem):
    size = mixed.shape[0] // PIECES
    moves = [(result, result_v, result_out)]
    for i in range(PIECES):
        rows = pl.ds(i * size, size)
        moves.append((mixed.at[rows], mixed_v.at[rows], mixed_out.at[rows]))
    reads = [pltpu.make_async_copy(a, b, sem.at[0, i]) for i, (a, b, _) in enumerate(moves)]
    writes = [pltpu.make_async_copy(b, c, sem.at[1, i]) for i, (_, b, c) in enumerate(moves)]
    for read in reads:
        read.start()
    for read, write in zip(reads, writes):
        read.wait()
        write.start()
    for write in writes:
        write.wait()


def local(n, audio_stream, audio_qkv, video_qkv, attention_out, norm_gain, weight_in, weight_out):
    tokens, width = audio_stream.shape
    chunks = width // LANES
    block = tokens * chunks
    audio = n * tokens
    video = video_qkv.shape[1]
    receivers = n * LANES // (audio * HEADS)
    part = HD // receivers + STATS
    vmem = pl.BlockSpec(memory_space=pltpu.VMEM)
    anywhere = pl.BlockSpec(memory_space=pltpu.HBM)
    hidden = weight_in.shape[1]
    gathered = pltpu.VMEM((n, block // 2, LANES), BF16)
    parts = pltpu.VMEM((n // 2, part, LANES), BF16)
    mixed, result = pl.pallas_call(
        functools.partial(kernel, n, math.gcd(n, NEAR)),
        out_shape=(
            jax.ShapeDtypeStruct((video, width), BF16),
            jax.ShapeDtypeStruct((tokens, width), BF16),
        ),
        in_specs=[anywhere] * 7,
        out_specs=(anywhere, vmem),
        scratch_shapes=[
            pltpu.VMEM(audio_stream.shape, BF16),
            pltpu.VMEM(audio_qkv.shape, BF16),
            pltpu.VMEM((chunks, LANES), F32),
            pltpu.VMEM((video, width), BF16),
            pltpu.VMEM((2 * video, width // 2), BF16),
            pltpu.VMEM((2 * video, width // 2), BF16),
            pltpu.VMEM((width // 2, 2 * video), BF16),
            pltpu.VMEM((2, attention_out.shape[0], width // 2), BF16),
            pltpu.VMEM((2, width // 2, hidden), BF16),
            pltpu.VMEM((2, hidden, width // 2), BF16),
            pltpu.VMEM((video, width), BF16),
            pltpu.VMEM((audio * chunks, LANES), F32),
            pltpu.VMEM((block, LANES), F32),
            pltpu.VMEM((audio, width // 2), BF16),
            pltpu.VMEM((audio, width), BF16),
            pltpu.VMEM((audio, width), BF16),
            pltpu.VMEM((2, audio, attention_out.shape[0]), BF16),
            pltpu.VMEM((2, audio, hidden), F32),
            pltpu.VMEM((2, audio, hidden), F32),
            pltpu.VMEM((2, block // 2, LANES), BF16),
            pltpu.VMEM((2, block // 2, LANES), BF16),
            pltpu.VMEM((n, block // 2, LANES), BF16),
            pltpu.VMEM((n, 2 * block, LANES), BF16),
            parts,
            parts,
            gathered,
            gathered,
            gathered,
            gathered,
            gathered,
            pltpu.SemaphoreType.DMA((9,)),
            pltpu.SemaphoreType.DMA,
            pltpu.SemaphoreType.DMA((14,)),
            pltpu.SemaphoreType.DMA((14,)),
        ],
        compiler_params=pltpu.CompilerParams(
            collective_id=0, has_side_effects=True, vmem_limit_bytes=60 * 1024 * 1024
        ),
        name="cross_modal_layer",
    )(
        audio_stream,
        audio_qkv,
        video_qkv,
        attention_out,
        norm_gain.reshape(chunks, LANES),
        weight_in,
        weight_out,
    )
    return pl.pallas_call(
        write_results,
        out_shape=(
            jax.ShapeDtypeStruct(mixed.shape, BF16),
            jax.ShapeDtypeStruct(result.shape, BF16),
        ),
        in_specs=[anywhere] * 2,
        out_specs=(anywhere, anywhere),
        scratch_shapes=[
            pltpu.VMEM(mixed.shape, BF16),
            pltpu.VMEM(result.shape, BF16),
            pltpu.SemaphoreType.DMA((2, PIECES + 1)),
        ],
        compiler_params=pltpu.CompilerParams(vmem_limit_bytes=60 * 1024 * 1024),
        name="write_results",
    )(mixed, result)


def solution(mesh):
    placed = (
        P(("groups", "seq"), None),
        P(None, ("groups", "seq"), None),
        P(None, ("groups", "seq"), None),
        P("seq", None),
        P(),
        P(None, "seq"),
        P("seq", None),
    )
    return jax.shard_map(
        functools.partial(local, mesh.shape["seq"]),
        mesh=mesh,
        in_specs=placed,
        out_specs=(P(("groups", "seq"), None), P(("groups", "seq"), None)),
        check_vma=False,
    )
```

```python
import functools
import math

import jax
import jax.numpy as jnp
from jax import lax
from jax.experimental import pallas as pl
from jax.experimental.pallas import tpu as pltpu
from jax.sharding import PartitionSpec as P

HEADS = 32
HD = 64
LANES = 128
STATS = 16
NEAR = 4
PIECES = 4
EPSILON = 1e-06
SCALE = 1.0 / math.sqrt(HD)
F32 = jnp.float32
BF16 = jnp.bfloat16


def mm(a, b, ca, cb):
    return lax.dot_general(a, b, (((ca,), (cb,)), ((), ())), preferred_element_type=F32)


def lane_of(shape):
    return lax.broadcasted_iota(jnp.int32, shape, len(shape) - 1)


def kernel(
    n, near, stream_in, aqkv_in, vqkv, wo, gain_in, w1, w2,
    vmix_out, result,
    stream, aqkv, gain, vq, vk, vv, vt, wo_v, w1_v, w2_v, vmix,
    relay, relay_own, qmat, kmat, vmat,
    attended_v, x_send, x_recv, mix_send, mix,
    q_send, g_q, g_kv, p_send, p_recv, a_send, a_recv, g_n, o_send, o_recv,
    load_sem, out_sem, send_sem, recv_sem,
):
    me = lax.axis_index("seq")
    tokens, width = stream_in.shape
    chunks = width // LANES
    block = tokens * chunks
    audio = n * tokens
    group = LANES // audio
    window = max(group * HD, LANES)
    windows = width // window
    subs = window // (group * HD)
    slab = wo.shape[0]
    receivers = n // (windows * subs)
    rows = HD // receivers

    def remote(src, dst, phase, peer):
        return pltpu.make_async_remote_copy(
            src_ref=src,
            dst_ref=dst,
            send_sem=send_sem.at[phase],
            recv_sem=recv_sem.at[phase],
            device_id={"seq": peer},
            device_id_type=pl.DeviceIdType.MESH,
        )

    def each_peer(act):
        for i in range(n - 1):
            act(lax.rem(me + 1 + (i + n // 2 - 1) % (n - 1), n))

    def each_chip(act):
        for i in range(1, n // 2):
            other = lax.rem(chip + (i + n // 4 - 1) % (n // 2 - 1) + 1, n // 2)
            act(other, other * 2 + core)

    def all_of(ref, phase, count=n - 1):
        part = ref.at[pl.ds(0, count)]
        return remote(part, part, phase, lax.rem(me + 1, n))

    barrier = pltpu.get_barrier_semaphore()
    each_peer(
        lambda peer: pl.semaphore_signal(
            barrier, inc=1, device_id={"seq": peer}, device_id_type=pl.DeviceIdType.MESH
        )
    )

    core = lax.rem(me, 2)
    chip = lax.div(me, 2)
    partner = me + 1 - 2 * core
    half = n // 2
    wide = width // 2
    mine = pl.ds(pl.multiple_of(core * wide, LANES), wide)
    theirs = pl.ds(pl.multiple_of((1 - core) * wide, LANES), wide)
    keys = vqkv.shape[1]
    first, second = pl.ds(0, keys), pl.ds(keys, keys)

    sources = (
        aqkv_in, vqkv.at[1, :, mine], vqkv.at[2, :, mine], vqkv.at[0], wo.at[:, mine],
        stream_in.at[:, mine], gain_in, w1.at[mine], w2.at[:, mine],
    )
    places = (
        aqkv, vk.at[first], vv.at[first], vq, wo_v.at[core],
        stream.at[core], gain, w1_v.at[core], w2_v.at[core],
    )
    loads = [
        pltpu.make_async_copy(src, dst, load_sem.at[i])
        for i, (src, dst) in enumerate(zip(sources, places))
    ]
    for load in loads:
        load.start()

    def own_rows(c, split):
        step = chunks // split
        return pl.ds(c // step * tokens * step + c % step, tokens, stride=step)

    def own_blocks(value, split=1):
        for c in range(chunks):
            relay_own[own_rows(c, split), :] = value[:, c * LANES : (c + 1) * LANES]
        return relay_own[...]

    far = n // near
    my_far, my_near = lax.div(me, near), lax.rem(me, near)
    kv_slot = my_near * far + my_far
    kv_row = pl.ds(my_near * far, far)

    def kv_across():
        for i in range(1, far):
            peer = lax.rem(my_far + i, far) * near + my_near
            remote(g_kv.at[kv_slot], g_kv.at[kv_slot], 1, peer).start()

    def kv_within():
        all_of(g_kv, 1, far - 1).wait_recv()
        for i in range(1, near):
            peer = my_far * near + lax.rem(my_near + i, near)
            remote(g_kv.at[kv_row], g_kv.at[kv_row], 6, peer).start()

    loads[0].wait()
    queries = own_blocks(aqkv[0].astype(F32), 2) * SCALE
    q_send[...] = queries.astype(BF16).reshape(q_send.shape)
    g_q[me] = q_send[core]
    g_kv[kv_slot, 0:block] = (own_blocks(aqkv[1].astype(F32)) * SCALE).astype(BF16)
    g_kv[kv_slot, block : 2 * block] = own_blocks(aqkv[2].astype(F32)).astype(BF16)

    pl.semaphore_wait(barrier, n - 1)
    shared = [
        remote(vqkv.at[1 + i, :, theirs], ref.at[second], 7 + i, partner)
        for i, ref in enumerate((vk, vv))
    ]
    for copy in shared:
        copy.start()
    each_peer(lambda peer: remote(q_send.at[lax.rem(peer, 2)], g_q.at[me], 0, peer).start())
    kv_across()

    def rows_of(blocks):
        count = blocks.shape[0] * blocks.shape[1]
        step = count // audio
        relay[0:count] = blocks.astype(F32).reshape(count, LANES)
        return jnp.concatenate(
            [relay[pl.ds(c, audio, stride=step), :].astype(BF16) for c in range(step)], axis=1
        )

    def blocks_of(value):
        step = chunks // 2
        for c in range(step):
            relay[pl.ds(c, audio, stride=step), :] = value[:, c * LANES : (c + 1) * LANES]
        return relay[0 : audio * step].astype(BF16).reshape(n, block // 2, LANES)

    def diagonal(part, sub):
        head = lane_of(part.shape) // HD
        return jnp.concatenate(
            [jnp.where(head == sub * group + h, part, jnp.zeros_like(part)) for h in range(group)],
            axis=0,
        )

    loads[1].wait()
    loads[2].wait()
    for copy in shared:
        copy.wait_recv()
    for w in range(windows // 2):
        cols = slice(w * window, (w + 1) * window)
        vt[cols, :] = vv[:, cols].T

    all_of(g_q, 0).wait_recv()
    qmat[...] = rows_of(g_q[...])

    for w in range(windows // 2):
        cols = slice(w * window, (w + 1) * window)
        for sub in range(subs):
            scores = mm(vk[:, cols], diagonal(qmat[:, cols], sub), 1, 1)
            peak = jnp.max(scores, axis=0, keepdims=True).astype(BF16).astype(F32)
            weights = jnp.exp(scores - peak)
            total = jnp.sum(weights, axis=0, keepdims=True)
            product = mm(vt[cols, :], weights.astype(BF16), 1, 0)
            lane = lane_of((HD, LANES)) // audio
            chosen = jnp.zeros((HD, LANES), F32)
            for h in range(group):
                at = (sub * group + h) * HD
                chosen = jnp.where(lane == h, product[at : at + HD], chosen)
            high = total.astype(BF16).astype(F32)
            row = lax.broadcasted_iota(jnp.int32, (STATS, LANES), 0)
            stats = jnp.where(
                row == 0, peak, jnp.where(row == 1, high, jnp.where(row == 2, total - high, 0.0))
            )
            for j in range(receivers):
                if slab < HD:
                    numerator, kept = chosen[j * rows : (j + 1) * rows], stats
                else:
                    span = slab // HD * audio
                    numerator, kept = jnp.zeros((rows, LANES), F32), jnp.zeros((STATS, LANES), F32)
                    for i in range(LANES // span):
                        shift = (i - j) * span % LANES
                        part, part_stats = chosen[i * rows : (i + 1) * rows], stats
                        if shift:
                            part = pltpu.roll(part, shift, 1)
                            part_stats = pltpu.roll(part_stats, shift, 1)
                        numerator = jnp.where(
                            lane_of((rows, LANES)) // span == i, part, numerator
                        )
                        kept = jnp.where(lane_of((STATS, LANES)) // span == i, part_stats, kept)
                target = (w * subs + sub) * receivers + j
                p_send[target, 0:rows] = numerator.astype(BF16)
                p_send[target, rows : rows + STATS] = kept.astype(BF16)

    for i in range(half):
        index = lax.rem(chip + (i + half // 2) % half, half)
        target = core * half + index

        @pl.when(me != target)
        def _():
            remote(p_send.at[index], p_recv.at[chip], 2, target).start()

    kv_within()
    weights_shared = [
        remote(stream_in.at[:, theirs], stream.at[core], 14, partner),
        remote(wo.at[:, theirs], wo_v.at[core], 9, partner),
        remote(w1.at[theirs], w1_v.at[core], 10, partner),
        remote(w2.at[:, theirs], w2_v.at[core], 11, partner),
    ]
    for copy in weights_shared:
        copy.start()
    own_part = lax.div(me, half) == core

    @pl.when(own_part)
    def _():
        p_recv[chip] = p_send[me - core * half]

    store = pltpu.make_async_copy(vmix, vmix_out, out_sem)

    def video(first, last):
        for w in range(first, last):
            cols = slice(w * window, (w + 1) * window)
            mixed = None
            for sub in range(subs):
                scores = mm(diagonal(kmat[:, cols], sub), vq[:, cols], 1, 1)
                scores = scores.reshape(group, audio, scores.shape[1])
                weights = jnp.exp(scores - jnp.max(scores, axis=1, keepdims=True))
                weights = weights / jnp.sum(weights, axis=1, keepdims=True)
                weights = weights.reshape(group * audio, scores.shape[2])
                term = mm(weights.T.astype(BF16), diagonal(vmat[:, cols], sub), 1, 0)
                mixed = term if mixed is None else mixed + term
            vmix[:, cols] = mixed.astype(BF16)

    @pl.when(own_part)
    def _():
        all_of(p_recv, 2, half - 1).wait_recv()

    @pl.when(jnp.logical_not(own_part))
    def _():
        all_of(p_recv, 2, half).wait_recv()

    parts = p_recv[...].astype(F32)
    peaks = parts[:, rows : rows + 1]
    scales = jnp.exp(peaks - jnp.max(peaks, axis=0, keepdims=True))
    totals = (parts[:, rows + 1 : rows + 2] + parts[:, rows + 2 : rows + 3]) * scales
    attended = jnp.sum(parts[:, 0:rows] * scales, axis=0) / jnp.sum(totals, axis=0)
    turned = attended.T.astype(BF16)
    if slab < HD:
        columns = turned
    else:
        heads = slab // HD
        folds = HD // rows
        columns = jnp.concatenate(
            [
                turned[(f * heads + h) * audio : (f * heads + h + 1) * audio]
                for h in range(heads)
                for f in range(folds)
            ],
            axis=1,
        )

    def scatter(value, send, recv, phase):
        send[...] = blocks_of(value)
        each_peer(lambda peer: remote(send.at[peer], recv.at[me], phase, peer).start())
        recv[me] = send[me]

    def gathered_sum(recv):
        return jnp.sum(recv[...].astype(F32).reshape(half, block, LANES), axis=0)

    step = chunks // 2

    attended_v[core] = columns
    swap = remote(attended_v.at[core], attended_v.at[core], 12, partner)
    swap.start()
    loads[4].wait()
    part = mm(columns, wo_v[core], 1, 0)
    weights_shared[1].wait_recv()
    swap.wait_recv()
    part = part + mm(attended_v[1 - core], wo_v[1 - core], 1, 0)
    a_send[...] = blocks_of(part).reshape(a_send.shape)
    each_chip(lambda other, peer: remote(a_send.at[other], a_recv.at[chip], 3, peer).start())
    a_recv[chip] = a_send[chip]
    loads[5].wait()
    loads[6].wait()
    weights_shared[0].wait_recv()
    for k in range(2):
        shown = stream[k].astype(F32)
        for c in range(step):
            relay_own[pl.ds(k * tokens * step + c, tokens, stride=step), :] = shown[
                :, c * LANES : (c + 1) * LANES
            ]
    own = relay_own[...]
    all_of(g_kv, 6, far * (near - 1)).wait_recv()
    loads[3].wait()
    kmat[...] = rows_of(g_kv[:, 0:block])
    vmat[...] = rows_of(g_kv[:, block : 2 * block])
    video(0, windows // 2)
    all_of(a_recv, 3, half - 1).wait_recv()
    mixed_audio = own + gathered_sum(a_recv)

    half_gain = gain[pl.ds(pl.multiple_of(core * step, step), step), :]
    scaled = mixed_audio.reshape(2 * tokens, step, LANES) * half_gain[None]
    g_n[chip] = scaled.reshape(block, LANES).astype(BF16)
    each_chip(lambda other, peer: remote(g_n.at[chip], g_n.at[chip], 4, peer).start())
    mix_send[...] = mixed_audio.reshape(2, block // 2, LANES)
    mix[core] = mix_send[core]
    exchange = remote(mix_send.at[1 - core], mix.at[core], 15, partner)
    exchange.start()
    video(windows // 2, windows)
    store.start()
    loads[7].wait()
    loads[8].wait()
    weights_shared[2].wait_recv()
    weights_shared[3].wait_recv()
    all_of(g_n, 4, half - 1).wait_recv()

    features = rows_of(g_n[...])
    units = w2.shape[0]
    for k in range(2):
        x_send[k, :, 0:units] = mm(features, w1_v[k], 1, 0)
    inverse = 1.0 / jnp.concatenate([half_gain[c : c + 1] for c in range(step)], axis=1)
    plain = features.astype(F32) * inverse
    square = jnp.sum(plain * plain, axis=1, keepdims=True)
    for k in range(2):
        x_send[k, :, units:] = jnp.broadcast_to(square, (audio, LANES))
    trade = remote(x_send, x_recv, 13, partner)
    trade.start()
    trade.wait_recv()
    square = (x_send[0, :, units:] + x_recv[0, :, units:])[:, 0:1]
    factor = lax.rsqrt(square / width + EPSILON)
    part = None
    for k in range(2):
        total = x_send[k, :, 0:units] + x_recv[k, :, 0:units]
        hidden = jax.nn.gelu(total * factor, approximate=True).astype(BF16)
        term = mm(hidden, w2_v[k], 1, 0)
        part = term if part is None else part + term
    scatter(part, o_send, o_recv, 5)
    all_of(o_recv, 5).wait_recv()
    exchange.wait_recv()
    relay_own[...] = mix[...].reshape(block, LANES) + gathered_sum(o_recv)
    for c in range(chunks):
        result[:, c * LANES : (c + 1) * LANES] = relay_own[own_rows(c, 2), :].astype(BF16)

    for copy in weights_shared + [swap, trade, exchange]:
        copy.wait_send()
    all_of(g_kv, 1, far - 1).wait_send()
    all_of(g_kv, 6, far * (near - 1)).wait_send()
    for copy in shared:
        copy.wait_send()

    @pl.when(own_part)
    def _():
        all_of(p_send, 2, half - 1).wait_send()

    @pl.when(jnp.logical_not(own_part))
    def _():
        all_of(p_send, 2, half).wait_send()

    for phase, ref in ((3, a_send), (4, g_n)):
        all_of(ref, phase, half - 1).wait_send()
    for phase, ref in ((0, g_q), (5, o_send)):
        all_of(ref, phase).wait_send()
    store.wait()


def write_results(mixed, result, mixed_out, result_out, mixed_v, result_v, sem):
    size = mixed.shape[0] // PIECES
    moves = [(result, result_v, result_out)]
    for i in range(PIECES):
        rows = pl.ds(i * size, size)
        moves.append((mixed.at[rows], mixed_v.at[rows], mixed_out.at[rows]))
    reads = [pltpu.make_async_copy(a, b, sem.at[0, i]) for i, (a, b, _) in enumerate(moves)]
    writes = [pltpu.make_async_copy(b, c, sem.at[1, i]) for i, (_, b, c) in enumerate(moves)]
    for read in reads:
        read.start()
    for read, write in zip(reads, writes):
        read.wait()
        write.start()
    for write in writes:
        write.wait()


def local(n, audio_stream, audio_qkv, video_qkv, attention_out, norm_gain, weight_in, weight_out):
    tokens, width = audio_stream.shape
    chunks = width // LANES
    block = tokens * chunks
    audio = n * tokens
    video = video_qkv.shape[1]
    receivers = n * LANES // (audio * HEADS)
    part = HD // receivers + STATS
    vmem = pl.BlockSpec(memory_space=pltpu.VMEM)
    anywhere = pl.BlockSpec(memory_space=pltpu.HBM)
    hidden = weight_in.shape[1]
    gathered = pltpu.VMEM((n, block // 2, LANES), BF16)
    by_chip = pltpu.VMEM((n // 2, block, LANES), BF16)
    parts = pltpu.VMEM((n // 2, part, LANES), BF16)
    mixed, result = pl.pallas_call(
        functools.partial(kernel, n, math.gcd(n, NEAR)),
        out_shape=(
            jax.ShapeDtypeStruct((video, width), BF16),
            jax.ShapeDtypeStruct((tokens, width), BF16),
        ),
        in_specs=[anywhere] * 7,
        out_specs=(anywhere, vmem),
        scratch_shapes=[
            pltpu.VMEM((2, tokens, width // 2), BF16),
            pltpu.VMEM(audio_qkv.shape, BF16),
            pltpu.VMEM((chunks, LANES), F32),
            pltpu.VMEM((video, width), BF16),
            pltpu.VMEM((2 * video, width // 2), BF16),
            pltpu.VMEM((2 * video, width // 2), BF16),
            pltpu.VMEM((width // 2, 2 * video), BF16),
            pltpu.VMEM((2, attention_out.shape[0], width // 2), BF16),
            pltpu.VMEM((2, width // 2, hidden), BF16),
            pltpu.VMEM((2, hidden, width // 2), BF16),
            pltpu.VMEM((video, width), BF16),
            pltpu.VMEM((audio * chunks, LANES), F32),
            pltpu.VMEM((block, LANES), F32),
            pltpu.VMEM((audio, width // 2), BF16),
            pltpu.VMEM((audio, width), BF16),
            pltpu.VMEM((audio, width), BF16),
            pltpu.VMEM((2, audio, attention_out.shape[0]), BF16),
            pltpu.VMEM((2, audio, hidden + LANES), F32),
            pltpu.VMEM((2, audio, hidden + LANES), F32),
            pltpu.VMEM((2, block // 2, LANES), F32),
            pltpu.VMEM((2, block // 2, LANES), F32),
            pltpu.VMEM((2, block // 2, LANES), BF16),
            pltpu.VMEM((n, block // 2, LANES), BF16),
            pltpu.VMEM((n, 2 * block, LANES), BF16),
            parts,
            parts,
            by_chip,
            by_chip,
            by_chip,
            gathered,
            gathered,
            pltpu.SemaphoreType.DMA((9,)),
            pltpu.SemaphoreType.DMA,
            pltpu.SemaphoreType.DMA((16,)),
            pltpu.SemaphoreType.DMA((16,)),
        ],
        compiler_params=pltpu.CompilerParams(
            collective_id=0, has_side_effects=True, vmem_limit_bytes=60 * 1024 * 1024
        ),
        name="cross_modal_layer",
    )(
        audio_stream,
        audio_qkv,
        video_qkv,
        attention_out,
        norm_gain.reshape(chunks, LANES),
        weight_in,
        weight_out,
    )
    return pl.pallas_call(
        write_results,
        out_shape=(
            jax.ShapeDtypeStruct(mixed.shape, BF16),
            jax.ShapeDtypeStruct(result.shape, BF16),
        ),
        in_specs=[anywhere] * 2,
        out_specs=(anywhere, anywhere),
        scratch_shapes=[
            pltpu.VMEM(mixed.shape, BF16),
            pltpu.VMEM(result.shape, BF16),
            pltpu.SemaphoreType.DMA((2, PIECES + 1)),
        ],
        compiler_params=pltpu.CompilerParams(vmem_limit_bytes=60 * 1024 * 1024),
        name="write_results",
    )(mixed, result)


def solution(mesh):
    placed = (
        P(("groups", "seq"), None),
        P(None, ("groups", "seq"), None),
        P(None, ("groups", "seq"), None),
        P("seq", None),
        P(),
        P(None, "seq"),
        P("seq", None),
    )
    return jax.shard_map(
        functools.partial(local, mesh.shape["seq"]),
        mesh=mesh,
        in_specs=placed,
        out_specs=(P(("groups", "seq"), None), P(("groups", "seq"), None)),
        check_vma=False,
    )
```

```python
import functools
import math

import jax
import jax.numpy as jnp
from jax import lax
from jax.experimental import pallas as pl
from jax.experimental.pallas import tpu as pltpu
from jax.sharding import PartitionSpec as P

HEADS = 32
HD = 64
LANES = 128
STATS = 16
NEAR = 4
PIECES = 4
EPSILON = 1e-06
SCALE = 1.0 / math.sqrt(HD)
F32 = jnp.float32
BF16 = jnp.bfloat16


def mm(a, b, ca, cb):
    return lax.dot_general(a, b, (((ca,), (cb,)), ((), ())), preferred_element_type=F32)


def lane_of(shape):
    return lax.broadcasted_iota(jnp.int32, shape, len(shape) - 1)


def kernel(
    n, near, stream_in, aqkv_in, vqkv, wo, gain_in, w1, w2,
    vmix_out, result,
    stream, aqkv, gain, vq, vk, vv, vt, wo_v, w1_v, w2_v, vmix,
    relay, relay_own, qmat, kmat, vmat,
    g_q, g_kv, p_send, p_recv, a_send, a_recv, g_n, o_send, o_recv,
    load_sem, out_sem, send_sem, recv_sem,
):
    me = lax.axis_index("seq")
    core, chip = lax.rem(me, 2), lax.div(me, 2)
    partner = me + 1 - 2 * core
    half = n // 2
    tokens, width = stream_in.shape
    chunks = width // LANES
    block = tokens * chunks
    keys = vqkv.shape[1]
    units = w2.shape[0]
    slab = 2 * wo.shape[0]
    audio = n * tokens
    asked = half * tokens

    def remote(src, dst, phase, peer):
        return pltpu.make_async_remote_copy(
            src_ref=src,
            dst_ref=dst,
            send_sem=send_sem.at[phase],
            recv_sem=recv_sem.at[phase],
            device_id={"seq": peer},
            device_id_type=pl.DeviceIdType.MESH,
        )

    def each_chip(act):
        for i in range(1, half):
            other = lax.rem(chip + (i + half // 2 - 1) % (half - 1) + 1, half)
            act(other, other * 2 + core)

    def all_of(ref, phase, count=half - 1):
        part = ref.at[pl.ds(0, count)]
        return remote(part, part, phase, partner)

    barrier = pltpu.get_barrier_semaphore()
    for i in range(1, n):
        pl.semaphore_signal(
            barrier,
            inc=1,
            device_id={"seq": lax.rem(me + i, n)},
            device_id_type=pl.DeviceIdType.MESH,
        )

    first, second = pl.ds(0, keys), pl.ds(keys, keys)
    wo_rows = pl.ds(pl.multiple_of(core * (slab // 2), slab // 2), slab // 2)
    sources = (aqkv_in, vqkv.at[1], vqkv.at[2], vqkv.at[0], wo, stream_in, gain_in, w1, w2)
    places = (
        aqkv, vk.at[first], vv.at[first], vq, wo_v.at[wo_rows],
        stream, gain, w1_v.at[core], w2_v.at[core],
    )
    loads = [
        pltpu.make_async_copy(src, dst, load_sem.at[i])
        for i, (src, dst) in enumerate(zip(sources, places))
    ]
    for load in loads:
        load.start()

    def own_blocks(value):
        for c in range(chunks):
            relay_own[pl.ds(c, tokens, stride=chunks), :] = value[:, c * LANES : (c + 1) * LANES]
        return relay_own[...]

    far = n // near
    my_far, my_near = lax.div(me, near), lax.rem(me, near)
    kv_slot = my_near * far + my_far
    kv_row = pl.ds(my_near * far, far)

    loads[0].wait()
    g_q[chip] = (own_blocks(aqkv[0].astype(F32)) * SCALE).astype(BF16)
    g_kv[kv_slot, 0:block] = (own_blocks(aqkv[1].astype(F32)) * SCALE).astype(BF16)
    g_kv[kv_slot, block : 2 * block] = own_blocks(aqkv[2].astype(F32)).astype(BF16)

    pl.semaphore_wait(barrier, n - 1)
    shared = [
        remote(vqkv.at[1], vk.at[second], 7, partner),
        remote(vqkv.at[2], vv.at[second], 8, partner),
        remote(wo, wo_v.at[wo_rows], 9, partner),
        remote(w1, w1_v.at[core], 10, partner),
        remote(w2, w2_v.at[core], 11, partner),
    ]
    for copy in shared[0:2]:
        copy.start()
    each_chip(lambda other, peer: remote(g_q.at[chip], g_q.at[chip], 0, peer).start())
    for i in range(1, far):
        peer = lax.rem(my_far + i, far) * near + my_near
        remote(g_kv.at[kv_slot], g_kv.at[kv_slot], 1, peer).start()

    def rows_of(blocks):
        step = chunks
        count = blocks.shape[0] * blocks.shape[1]
        relay[0:count] = blocks.astype(F32).reshape(count, LANES)
        return jnp.concatenate(
            [
                relay[pl.ds(c, count // step, stride=step), :].astype(BF16)
                for c in range(step)
            ],
            axis=1,
        )

    def blocks_of(value):
        for c in range(chunks):
            relay[pl.ds(c, asked, stride=chunks), :] = value[:, c * LANES : (c + 1) * LANES]
        return relay[0 : asked * chunks].astype(BF16).reshape(half, block, LANES)

    def scatter(value, send, recv, phase):
        send[...] = blocks_of(value)
        each_chip(lambda other, peer: remote(send.at[other], recv.at[chip], phase, peer).start())
        recv[chip] = send[chip]

    def gathered_sum(recv):
        return jnp.sum(recv[...].astype(F32), axis=0)

    def diagonal(part, sub, group):
        head = lane_of(part.shape) // HD
        return jnp.concatenate(
            [jnp.where(head == sub * group + h, part, jnp.zeros_like(part)) for h in range(group)],
            axis=0,
        )

    def windows_of(rows):
        group = LANES // rows
        window = max(group * HD, LANES)
        return group, window, width // window, window // (group * HD)

    group, window, windows, subs = windows_of(asked)
    receivers = half // (windows * subs)
    rows = HD // receivers

    loads[1].wait()
    loads[2].wait()
    for copy in shared[0:2]:
        copy.wait_recv()
    for w in range(windows):
        cols = slice(w * window, (w + 1) * window)
        vt[cols, :] = vv[:, cols].T

    all_of(g_q, 0).wait_recv()
    qmat[...] = rows_of(g_q[...])

    for w in range(windows):
        cols = slice(w * window, (w + 1) * window)
        for sub in range(subs):
            scores = mm(vk[:, cols], diagonal(qmat[:, cols], sub, group), 1, 1)
            peak = jnp.max(scores, axis=0, keepdims=True).astype(BF16).astype(F32)
            weights = jnp.exp(scores - peak)
            total = jnp.sum(weights, axis=0, keepdims=True)
            product = mm(vt[cols, :], weights.astype(BF16), 1, 0)
            lane = lane_of((HD, LANES)) // asked
            chosen = jnp.zeros((HD, LANES), F32)
            for h in range(group):
                at = (sub * group + h) * HD
                chosen = jnp.where(lane == h, product[at : at + HD], chosen)
            high = total.astype(BF16).astype(F32)
            row = lax.broadcasted_iota(jnp.int32, (STATS, LANES), 0)
            stats = jnp.where(
                row == 0, peak, jnp.where(row == 1, high, jnp.where(row == 2, total - high, 0.0))
            )
            for j in range(receivers):
                if slab < HD:
                    numerator, kept = chosen[j * rows : (j + 1) * rows], stats
                else:
                    span = slab // HD * asked
                    numerator, kept = jnp.zeros((rows, LANES), F32), jnp.zeros((STATS, LANES), F32)
                    for i in range(LANES // span):
                        shift = (i - j) * span % LANES
                        part, part_stats = chosen[i * rows : (i + 1) * rows], stats
                        if shift:
                            part = pltpu.roll(part, shift, 1)
                            part_stats = pltpu.roll(part_stats, shift, 1)
                        numerator = jnp.where(
                            lane_of((rows, LANES)) // span == i, part, numerator
                        )
                        kept = jnp.where(lane_of((STATS, LANES)) // span == i, part_stats, kept)
                target = (w * subs + sub) * receivers + j
                p_send[target, 0:rows] = numerator.astype(BF16)
                p_send[target, rows : rows + STATS] = kept.astype(BF16)

    each_chip(lambda other, peer: remote(p_send.at[other], p_recv.at[chip], 2, peer).start())
    all_of(g_kv, 1, far - 1).wait_recv()
    for i in range(1, near):
        peer = my_far * near + lax.rem(my_near + i, near)
        remote(g_kv.at[kv_row], g_kv.at[kv_row], 6, peer).start()
    for copy in shared[2:]:
        copy.start()
    p_recv[chip] = p_send[chip]

    store = pltpu.make_async_copy(vmix, vmix_out, out_sem)
    v_group, v_window, v_windows, v_subs = windows_of(audio)

    def video(start, stop):
        for w in range(start, stop):
            cols = slice(w * v_window, (w + 1) * v_window)
            mixed = None
            for sub in range(v_subs):
                scores = mm(diagonal(kmat[:, cols], sub, v_group), vq[:, cols], 1, 1)
                scores = scores.reshape(v_group, audio, scores.shape[1])
                weights = jnp.exp(scores - jnp.max(scores, axis=1, keepdims=True))
                weights = weights * (1.0 / jnp.sum(weights, axis=1, keepdims=True))
                weights = weights.reshape(v_group * audio, scores.shape[2])
                term = mm(weights.T.astype(BF16), diagonal(vmat[:, cols], sub, v_group), 1, 0)
                mixed = term if mixed is None else mixed + term
            vmix[:, cols] = mixed.astype(BF16)

    all_of(p_recv, 2).wait_recv()
    parts = p_recv[...].astype(F32)
    peaks = parts[:, rows : rows + 1]
    scales = jnp.exp(peaks - jnp.max(peaks, axis=0, keepdims=True))
    totals = (parts[:, rows + 1 : rows + 2] + parts[:, rows + 2 : rows + 3]) * scales
    attended = jnp.sum(parts[:, 0:rows] * scales, axis=0) / jnp.sum(totals, axis=0)
    turned = attended.T.astype(BF16)
    if slab < HD:
        columns = turned
    else:
        heads = slab // HD
        folds = HD // rows
        columns = jnp.concatenate(
            [
                turned[(f * heads + h) * asked : (f * heads + h + 1) * asked]
                for h in range(heads)
                for f in range(folds)
            ],
            axis=1,
        )

    loads[4].wait()
    shared[2].wait_recv()
    scatter(mm(columns, wo_v[...], 1, 0), a_send, a_recv, 3)
    loads[5].wait()
    loads[6].wait()
    own = own_blocks(stream[...].astype(F32))
    all_of(g_kv, 6, far * (near - 1)).wait_recv()
    loads[3].wait()
    kmat[...] = rows_of(g_kv[:, 0:block])
    vmat[...] = rows_of(g_kv[:, block : 2 * block])
    video(0, v_windows // 2)
    all_of(a_recv, 3).wait_recv()
    mixed_audio = own + gathered_sum(a_recv)

    by_token = mixed_audio.reshape(tokens, chunks, LANES)
    square = jnp.sum(jnp.sum(by_token * by_token, axis=1, keepdims=True), axis=2, keepdims=True)
    normed = by_token * lax.rsqrt(square / width + EPSILON) * gain[...][None]
    g_n[chip] = normed.reshape(block, LANES).astype(BF16)
    each_chip(lambda other, peer: remote(g_n.at[chip], g_n.at[chip], 4, peer).start())
    video(v_windows // 2, v_windows)
    store.start()
    loads[7].wait()
    loads[8].wait()
    shared[3].wait_recv()
    shared[4].wait_recv()
    all_of(g_n, 4).wait_recv()

    features = rows_of(g_n[...])
    part = None
    for k in range(2):
        hidden = jax.nn.gelu(mm(features, w1_v[k], 1, 0), approximate=True).astype(BF16)
        term = mm(hidden, w2_v[k], 1, 0)
        part = term if part is None else part + term
    scatter(part, o_send, o_recv, 5)
    all_of(o_recv, 5).wait_recv()
    relay_own[...] = mixed_audio + gathered_sum(o_recv)
    for c in range(chunks):
        result[:, c * LANES : (c + 1) * LANES] = relay_own[
            pl.ds(c, tokens, stride=chunks), :
        ].astype(BF16)

    for copy in shared:
        copy.wait_send()
    all_of(g_kv, 1, far - 1).wait_send()
    all_of(g_kv, 6, far * (near - 1)).wait_send()
    for phase, ref in ((0, g_q), (2, p_send), (3, a_send), (4, g_n), (5, o_send)):
        all_of(ref, phase).wait_send()
    store.wait()


def write_results(mixed, result, mixed_out, result_out, mixed_v, result_v, sem):
    size = mixed.shape[0] // PIECES
    moves = [(result, result_v, result_out)]
    for i in range(PIECES):
        rows = pl.ds(i * size, size)
        moves.append((mixed.at[rows], mixed_v.at[rows], mixed_out.at[rows]))
    reads = [pltpu.make_async_copy(a, b, sem.at[0, i]) for i, (a, b, _) in enumerate(moves)]
    writes = [pltpu.make_async_copy(b, c, sem.at[1, i]) for i, (_, b, c) in enumerate(moves)]
    for read in reads:
        read.start()
    for read, write in zip(reads, writes):
        read.wait()
        write.start()
    for write in writes:
        write.wait()


def local(n, audio_stream, audio_qkv, video_qkv, attention_out, norm_gain, weight_in, weight_out):
    tokens, width = audio_stream.shape
    chunks = width // LANES
    block = tokens * chunks
    audio = n * tokens
    video = video_qkv.shape[1]
    asked = audio // 2
    receivers = n // 2 * LANES // (asked * HEADS)
    part = HD // receivers + STATS
    hidden = weight_in.shape[1]
    slab = attention_out.shape[0]
    anywhere = pl.BlockSpec(memory_space=pltpu.HBM)
    vmem = pl.BlockSpec(memory_space=pltpu.VMEM)
    by_chip = pltpu.VMEM((n // 2, block, LANES), BF16)
    parts = pltpu.VMEM((n // 2, part, LANES), BF16)
    mixed, result = pl.pallas_call(
        functools.partial(kernel, n, math.gcd(n, NEAR)),
        out_shape=(
            jax.ShapeDtypeStruct((video, width), BF16),
            jax.ShapeDtypeStruct((tokens, width), BF16),
        ),
        in_specs=[anywhere] * 7,
        out_specs=(anywhere, vmem),
        scratch_shapes=[
            pltpu.VMEM(audio_stream.shape, BF16),
            pltpu.VMEM(audio_qkv.shape, BF16),
            pltpu.VMEM((chunks, LANES), F32),
            pltpu.VMEM((video, width), BF16),
            pltpu.VMEM((2 * video, width), BF16),
            pltpu.VMEM((2 * video, width), BF16),
            pltpu.VMEM((width, 2 * video), BF16),
            pltpu.VMEM((2 * slab, width), BF16),
            pltpu.VMEM((2, width, hidden), BF16),
            pltpu.VMEM((2, hidden, width), BF16),
            pltpu.VMEM((video, width), BF16),
            pltpu.VMEM((audio * chunks, LANES), F32),
            pltpu.VMEM((block, LANES), F32),
            pltpu.VMEM((asked, width), BF16),
            pltpu.VMEM((audio, width), BF16),
            pltpu.VMEM((audio, width), BF16),
            by_chip,
            pltpu.VMEM((n, 2 * block, LANES), BF16),
            parts,
            parts,
            by_chip,
            by_chip,
            by_chip,
            by_chip,
            by_chip,
            pltpu.SemaphoreType.DMA((9,)),
            pltpu.SemaphoreType.DMA,
            pltpu.SemaphoreType.DMA((12,)),
            pltpu.SemaphoreType.DMA((12,)),
        ],
        compiler_params=pltpu.CompilerParams(
            collective_id=0, has_side_effects=True, vmem_limit_bytes=60 * 1024 * 1024
        ),
        name="cross_modal_layer",
    )(
        audio_stream,
        audio_qkv,
        video_qkv,
        attention_out,
        norm_gain.reshape(chunks, LANES),
        weight_in,
        weight_out,
    )
    return pl.pallas_call(
        write_results,
        out_shape=(
            jax.ShapeDtypeStruct(mixed.shape, BF16),
            jax.ShapeDtypeStruct(result.shape, BF16),
        ),
        in_specs=[anywhere] * 2,
        out_specs=(anywhere, anywhere),
        scratch_shapes=[
            pltpu.VMEM(mixed.shape, BF16),
            pltpu.VMEM(result.shape, BF16),
            pltpu.SemaphoreType.DMA((2, PIECES + 1)),
        ],
        compiler_params=pltpu.CompilerParams(vmem_limit_bytes=60 * 1024 * 1024),
        name="write_results",
    )(mixed, result)


def solution(mesh):
    placed = (
        P(("groups", "seq"), None),
        P(None, ("groups", "seq"), None),
        P(None, ("groups", "seq"), None),
        P("seq", None),
        P(),
        P(None, "seq"),
        P("seq", None),
    )
    return jax.shard_map(
        functools.partial(local, mesh.shape["seq"]),
        mesh=mesh,
        in_specs=placed,
        out_specs=(P(("groups", "seq"), None), P(("groups", "seq"), None)),
        check_vma=False,
    )
```

```python
import functools
import math

import jax
import jax.numpy as jnp
from jax import lax
from jax.experimental import pallas as pl
from jax.experimental.pallas import tpu as pltpu
from jax.sharding import PartitionSpec as P

HEADS = 32
HD = 64
LANES = 128
STATS = 16
NEAR = 4
PIECES = 4
EPSILON = 1e-06
SCALE = 1.0 / math.sqrt(HD)
F32 = jnp.float32
BF16 = jnp.bfloat16


def mm(a, b, ca, cb):
    return lax.dot_general(a, b, (((ca,), (cb,)), ((), ())), preferred_element_type=F32)


def lane_of(shape):
    return lax.broadcasted_iota(jnp.int32, shape, len(shape) - 1)


def kernel(
    n, near, stream_in, aqkv_in, vqkv, wo, gain_in, w1, w2,
    vmix_out, result,
    stream, aqkv, gain, vq, vk, vv, vt, wo_v, w1_v, w2_v, vmix,
    relay, relay_own, qmat, kmat, vmat,
    g_q, g_kv, p_send, p_recv, a_send, a_recv, g_n, o_send, o_recv,
    load_sem, out_sem, send_sem, recv_sem,
):
    me = lax.axis_index("seq")
    core, chip = lax.rem(me, 2), lax.div(me, 2)
    partner = me + 1 - 2 * core
    half = n // 2
    tokens, width = stream_in.shape
    chunks = width // LANES
    block = tokens * chunks
    keys = vqkv.shape[1]
    units = w2.shape[0]
    slab = 2 * wo.shape[0]
    audio = n * tokens
    asked = half * tokens

    def remote(src, dst, phase, peer):
        return pltpu.make_async_remote_copy(
            src_ref=src,
            dst_ref=dst,
            send_sem=send_sem.at[phase],
            recv_sem=recv_sem.at[phase],
            device_id={"seq": peer},
            device_id_type=pl.DeviceIdType.MESH,
        )

    def each_chip(act):
        for i in range(1, half):
            other = lax.rem(chip + (i + half // 2 - 1) % (half - 1) + 1, half)
            act(other, other * 2 + core)

    def all_of(ref, phase, count=half - 1):
        part = ref.at[pl.ds(0, count)]
        return remote(part, part, phase, partner)

    barrier = pltpu.get_barrier_semaphore()
    for i in range(1, n):
        pl.semaphore_signal(
            barrier,
            inc=1,
            device_id={"seq": lax.rem(me + i, n)},
            device_id_type=pl.DeviceIdType.MESH,
        )

    first, second = pl.ds(0, keys), pl.ds(keys, keys)
    wo_rows = pl.ds(pl.multiple_of(core * (slab // 2), slab // 2), slab // 2)
    sources = (aqkv_in, vqkv.at[1], vqkv.at[2], vqkv.at[0], wo, stream_in, gain_in, w1, w2)
    places = (
        aqkv, vk.at[first], vv.at[first], vq, wo_v.at[wo_rows],
        stream, gain, w1_v.at[core], w2_v.at[core],
    )
    loads = [
        pltpu.make_async_copy(src, dst, load_sem.at[i])
        for i, (src, dst) in enumerate(zip(sources, places))
    ]
    for load in loads:
        load.start()

    def own_blocks(value):
        for c in range(chunks):
            relay_own[pl.ds(c, tokens, stride=chunks), :] = value[:, c * LANES : (c + 1) * LANES]
        return relay_own[...]

    far = n // near
    my_far, my_near = lax.div(me, near), lax.rem(me, near)
    kv_slot = my_near * far + my_far
    kv_row = pl.ds(my_near * far, far)

    loads[0].wait()
    g_q[chip] = (own_blocks(aqkv[0].astype(F32)) * SCALE).astype(BF16)
    g_kv[kv_slot, 0:block] = (own_blocks(aqkv[1].astype(F32)) * SCALE).astype(BF16)
    g_kv[kv_slot, block : 2 * block] = own_blocks(aqkv[2].astype(F32)).astype(BF16)

    pl.semaphore_wait(barrier, n - 1)
    shared = [
        remote(vqkv.at[1], vk.at[second], 7, partner),
        remote(vqkv.at[2], vv.at[second], 8, partner),
        remote(wo, wo_v.at[wo_rows], 9, partner),
        remote(w1, w1_v.at[core], 10, partner),
        remote(w2, w2_v.at[core], 11, partner),
    ]
    for copy in shared[0:2]:
        copy.start()
    each_chip(lambda other, peer: remote(g_q.at[chip], g_q.at[chip], 0, peer).start())
    for i in range(1, far):
        peer = lax.rem(my_far + i, far) * near + my_near
        remote(g_kv.at[kv_slot], g_kv.at[kv_slot], 1, peer).start()

    def rows_of(blocks):
        step = chunks
        count = blocks.shape[0] * blocks.shape[1]
        relay[0:count] = blocks.astype(F32).reshape(count, LANES)
        return jnp.concatenate(
            [
                relay[pl.ds(c, count // step, stride=step), :].astype(BF16)
                for c in range(step)
            ],
            axis=1,
        )

    def blocks_of(value):
        for c in range(chunks):
            relay[pl.ds(c, asked, stride=chunks), :] = value[:, c * LANES : (c + 1) * LANES]
        return relay[0 : asked * chunks].astype(BF16).reshape(half, block, LANES)

    def scatter(value, send, recv, phase):
        send[...] = blocks_of(value)
        each_chip(lambda other, peer: remote(send.at[other], recv.at[chip], phase, peer).start())
        recv[chip] = send[chip]

    def gathered_sum(recv):
        return jnp.sum(recv[...].astype(F32), axis=0)

    def diagonal(part, sub, group):
        head = lane_of(part.shape) // HD
        return jnp.concatenate(
            [jnp.where(head == sub * group + h, part, jnp.zeros_like(part)) for h in range(group)],
            axis=0,
        )

    def windows_of(rows):
        group = LANES // rows
        window = max(group * HD, LANES)
        return group, window, width // window, window // (group * HD)

    group, window, windows, subs = windows_of(asked)
    receivers = half // (windows * subs)
    rows = HD // receivers

    loads[1].wait()
    loads[2].wait()
    for copy in shared[0:2]:
        copy.wait_recv()
    for copy in shared[2:]:
        copy.start()
    for w in range(windows):
        cols = slice(w * window, (w + 1) * window)
        vt[cols, :] = vv[:, cols].T

    all_of(g_q, 0).wait_recv()
    qmat[...] = rows_of(g_q[...])

    for w in range(windows):
        cols = slice(w * window, (w + 1) * window)
        for sub in range(subs):
            scores = mm(vk[:, cols], diagonal(qmat[:, cols], sub, group), 1, 1)
            peak = jnp.max(scores, axis=0, keepdims=True).astype(BF16).astype(F32)
            weights = jnp.exp(scores - peak)
            total = jnp.sum(weights, axis=0, keepdims=True)
            product = mm(vt[cols, :], weights.astype(BF16), 1, 0)
            lane = lane_of((HD, LANES)) // asked
            chosen = jnp.zeros((HD, LANES), F32)
            for h in range(group):
                at = (sub * group + h) * HD
                chosen = jnp.where(lane == h, product[at : at + HD], chosen)
            high = total.astype(BF16).astype(F32)
            row = lax.broadcasted_iota(jnp.int32, (STATS, LANES), 0)
            stats = jnp.where(
                row == 0, peak, jnp.where(row == 1, high, jnp.where(row == 2, total - high, 0.0))
            )
            for j in range(receivers):
                if slab < HD:
                    numerator, kept = chosen[j * rows : (j + 1) * rows], stats
                else:
                    span = slab // HD * asked
                    numerator, kept = jnp.zeros((rows, LANES), F32), jnp.zeros((STATS, LANES), F32)
                    for i in range(LANES // span):
                        shift = (i - j) * span % LANES
                        part, part_stats = chosen[i * rows : (i + 1) * rows], stats
                        if shift:
                            part = pltpu.roll(part, shift, 1)
                            part_stats = pltpu.roll(part_stats, shift, 1)
                        numerator = jnp.where(
                            lane_of((rows, LANES)) // span == i, part, numerator
                        )
                        kept = jnp.where(lane_of((STATS, LANES)) // span == i, part_stats, kept)
                target = (w * subs + sub) * receivers + j
                p_send[target, 0:rows] = numerator.astype(BF16)
                p_send[target, rows : rows + STATS] = kept.astype(BF16)

    each_chip(lambda other, peer: remote(p_send.at[other], p_recv.at[chip], 2, peer).start())
    all_of(g_kv, 1, far - 1).wait_recv()
    for i in range(1, near):
        peer = my_far * near + lax.rem(my_near + i, near)
        remote(g_kv.at[kv_row], g_kv.at[kv_row], 6, peer).start()
    p_recv[chip] = p_send[chip]

    store = pltpu.make_async_copy(vmix, vmix_out, out_sem)
    v_group, v_window, v_windows, v_subs = windows_of(audio)

    def video(start, stop):
        for w in range(start, stop):
            cols = slice(w * v_window, (w + 1) * v_window)
            mixed = None
            for sub in range(v_subs):
                scores = mm(diagonal(kmat[:, cols], sub, v_group), vq[:, cols], 1, 1)
                scores = scores.reshape(v_group, audio, scores.shape[1])
                weights = jnp.exp(scores - jnp.max(scores, axis=1, keepdims=True))
                weights = weights * (1.0 / jnp.sum(weights, axis=1, keepdims=True))
                weights = weights.reshape(v_group * audio, scores.shape[2])
                term = mm(weights.T.astype(BF16), diagonal(vmat[:, cols], sub, v_group), 1, 0)
                mixed = term if mixed is None else mixed + term
            vmix[:, cols] = mixed.astype(BF16)

    all_of(p_recv, 2).wait_recv()
    parts = p_recv[...].astype(F32)
    peaks = parts[:, rows : rows + 1]
    scales = jnp.exp(peaks - jnp.max(peaks, axis=0, keepdims=True))
    totals = (parts[:, rows + 1 : rows + 2] + parts[:, rows + 2 : rows + 3]) * scales
    attended = jnp.sum(parts[:, 0:rows] * scales, axis=0) / jnp.sum(totals, axis=0)
    turned = attended.T.astype(BF16)
    if slab < HD:
        columns = turned
    else:
        heads = slab // HD
        folds = HD // rows
        columns = jnp.concatenate(
            [
                turned[(f * heads + h) * asked : (f * heads + h + 1) * asked]
                for h in range(heads)
                for f in range(folds)
            ],
            axis=1,
        )

    loads[4].wait()
    shared[2].wait_recv()
    scatter(mm(columns, wo_v[...], 1, 0), a_send, a_recv, 3)
    loads[5].wait()
    loads[6].wait()
    own = own_blocks(stream[...].astype(F32))
    all_of(g_kv, 6, far * (near - 1)).wait_recv()
    loads[3].wait()
    kmat[...] = rows_of(g_kv[:, 0:block])
    vmat[...] = rows_of(g_kv[:, block : 2 * block])
    video(0, v_windows // 2)
    all_of(a_recv, 3).wait_recv()
    mixed_audio = own + gathered_sum(a_recv)

    by_token = mixed_audio.reshape(tokens, chunks, LANES)
    square = jnp.sum(jnp.sum(by_token * by_token, axis=1, keepdims=True), axis=2, keepdims=True)
    normed = by_token * lax.rsqrt(square / width + EPSILON) * gain[...][None]
    g_n[chip] = normed.reshape(block, LANES).astype(BF16)
    each_chip(lambda other, peer: remote(g_n.at[chip], g_n.at[chip], 4, peer).start())
    video(v_windows // 2, v_windows)
    store.start()
    loads[7].wait()
    loads[8].wait()
    all_of(g_n, 4).wait_recv()

    features = rows_of(g_n[...])
    hidden = []
    for k in range(2):
        if k:
            shared[3].wait_recv()
        opened = mm(features, w1_v[core if k == 0 else 1 - core], 1, 0)
        hidden.append(jax.nn.gelu(opened, approximate=True).astype(BF16))
    part = mm(hidden[0], w2_v[core], 1, 0)
    shared[4].wait_recv()
    part = part + mm(hidden[1], w2_v[1 - core], 1, 0)
    scatter(part, o_send, o_recv, 5)
    all_of(o_recv, 5).wait_recv()
    relay_own[...] = mixed_audio + gathered_sum(o_recv)
    for c in range(chunks):
        result[:, c * LANES : (c + 1) * LANES] = relay_own[
            pl.ds(c, tokens, stride=chunks), :
        ].astype(BF16)

    for copy in shared:
        copy.wait_send()
    all_of(g_kv, 1, far - 1).wait_send()
    all_of(g_kv, 6, far * (near - 1)).wait_send()
    for phase, ref in ((0, g_q), (2, p_send), (3, a_send), (4, g_n), (5, o_send)):
        all_of(ref, phase).wait_send()
    store.wait()


def write_results(mixed, result, mixed_out, result_out, mixed_v, result_v, sem):
    size = mixed.shape[0] // PIECES
    moves = [(result, result_v, result_out)]
    for i in range(PIECES):
        rows = pl.ds(i * size, size)
        moves.append((mixed.at[rows], mixed_v.at[rows], mixed_out.at[rows]))
    reads = [pltpu.make_async_copy(a, b, sem.at[0, i]) for i, (a, b, _) in enumerate(moves)]
    writes = [pltpu.make_async_copy(b, c, sem.at[1, i]) for i, (_, b, c) in enumerate(moves)]
    for read in reads:
        read.start()
    for read, write in zip(reads, writes):
        read.wait()
        write.start()
    for write in writes:
        write.wait()


def local(n, audio_stream, audio_qkv, video_qkv, attention_out, norm_gain, weight_in, weight_out):
    tokens, width = audio_stream.shape
    chunks = width // LANES
    block = tokens * chunks
    audio = n * tokens
    video = video_qkv.shape[1]
    asked = audio // 2
    receivers = n // 2 * LANES // (asked * HEADS)
    part = HD // receivers + STATS
    hidden = weight_in.shape[1]
    slab = attention_out.shape[0]
    anywhere = pl.BlockSpec(memory_space=pltpu.HBM)
    vmem = pl.BlockSpec(memory_space=pltpu.VMEM)
    by_chip = pltpu.VMEM((n // 2, block, LANES), BF16)
    parts = pltpu.VMEM((n // 2, part, LANES), BF16)
    mixed, result = pl.pallas_call(
        functools.partial(kernel, n, math.gcd(n, NEAR)),
        out_shape=(
            jax.ShapeDtypeStruct((video, width), BF16),
            jax.ShapeDtypeStruct((tokens, width), BF16),
        ),
        in_specs=[anywhere] * 7,
        out_specs=(anywhere, vmem),
        scratch_shapes=[
            pltpu.VMEM(audio_stream.shape, BF16),
            pltpu.VMEM(audio_qkv.shape, BF16),
            pltpu.VMEM((chunks, LANES), F32),
            pltpu.VMEM((video, width), BF16),
            pltpu.VMEM((2 * video, width), BF16),
            pltpu.VMEM((2 * video, width), BF16),
            pltpu.VMEM((width, 2 * video), BF16),
            pltpu.VMEM((2 * slab, width), BF16),
            pltpu.VMEM((2, width, hidden), BF16),
            pltpu.VMEM((2, hidden, width), BF16),
            pltpu.VMEM((video, width), BF16),
            pltpu.VMEM((audio * chunks, LANES), F32),
            pltpu.VMEM((block, LANES), F32),
            pltpu.VMEM((asked, width), BF16),
            pltpu.VMEM((audio, width), BF16),
            pltpu.VMEM((audio, width), BF16),
            by_chip,
            pltpu.VMEM((n, 2 * block, LANES), BF16),
            parts,
            parts,
            by_chip,
            by_chip,
            by_chip,
            by_chip,
            by_chip,
            pltpu.SemaphoreType.DMA((9,)),
            pltpu.SemaphoreType.DMA,
            pltpu.SemaphoreType.DMA((12,)),
            pltpu.SemaphoreType.DMA((12,)),
        ],
        compiler_params=pltpu.CompilerParams(
            collective_id=0, has_side_effects=True, vmem_limit_bytes=60 * 1024 * 1024
        ),
        name="cross_modal_layer",
    )(
        audio_stream,
        audio_qkv,
        video_qkv,
        attention_out,
        norm_gain.reshape(chunks, LANES),
        weight_in,
        weight_out,
    )
    return pl.pallas_call(
        write_results,
        out_shape=(
            jax.ShapeDtypeStruct(mixed.shape, BF16),
            jax.ShapeDtypeStruct(result.shape, BF16),
        ),
        in_specs=[anywhere] * 2,
        out_specs=(anywhere, anywhere),
        scratch_shapes=[
            pltpu.VMEM(mixed.shape, BF16),
            pltpu.VMEM(result.shape, BF16),
            pltpu.SemaphoreType.DMA((2, PIECES + 1)),
        ],
        compiler_params=pltpu.CompilerParams(vmem_limit_bytes=60 * 1024 * 1024),
        name="write_results",
    )(mixed, result)


def solution(mesh):
    placed = (
        P(("groups", "seq"), None),
        P(None, ("groups", "seq"), None),
        P(None, ("groups", "seq"), None),
        P("seq", None),
        P(),
        P(None, "seq"),
        P("seq", None),
    )
    return jax.shard_map(
        functools.partial(local, mesh.shape["seq"]),
        mesh=mesh,
        in_specs=placed,
        out_specs=(P(("groups", "seq"), None), P(("groups", "seq"), None)),
        check_vma=False,
    )
```

```python
import functools
import math

import jax
import jax.numpy as jnp
from jax import lax
from jax.experimental import pallas as pl
from jax.experimental.pallas import tpu as pltpu
from jax.sharding import PartitionSpec as P

HEADS = 32
HD = 64
LANES = 128
STATS = 16
NEAR = 4
PIECES = 4
EPSILON = 1e-06
SCALE = 1.0 / math.sqrt(HD)
F32 = jnp.float32
BF16 = jnp.bfloat16


def mm(a, b, ca, cb):
    return lax.dot_general(a, b, (((ca,), (cb,)), ((), ())), preferred_element_type=F32)


def lane_of(shape):
    return lax.broadcasted_iota(jnp.int32, shape, len(shape) - 1)


def kernel(
    n, near, stream_in, aqkv_in, vqkv, wo, gain_in, w1, w2,
    vmix_out, result,
    stream, aqkv, gain, vq, vk, vv, vt, wo_v, w1_v, w2_v, vmix,
    relay, relay_own, qmat, kmat, vmat, logits, rounded,
    g_q, g_kv, p_send, p_recv, a_send, a_recv, g_n, o_send, o_recv,
    load_sem, out_sem, send_sem, recv_sem,
):
    me = lax.axis_index("seq")
    core, chip = lax.rem(me, 2), lax.div(me, 2)
    partner = me + 1 - 2 * core
    half = n // 2
    tokens, width = stream_in.shape
    chunks = width // LANES
    block = tokens * chunks
    keys = vqkv.shape[1]
    units = w2.shape[0]
    slab = 2 * wo.shape[0]
    audio = n * tokens
    asked = half * tokens

    def remote(src, dst, phase, peer):
        return pltpu.make_async_remote_copy(
            src_ref=src,
            dst_ref=dst,
            send_sem=send_sem.at[phase],
            recv_sem=recv_sem.at[phase],
            device_id={"seq": peer},
            device_id_type=pl.DeviceIdType.MESH,
        )

    def each_chip(act):
        for i in range(1, half):
            other = lax.rem(chip + (i + half // 2 - 1) % (half - 1) + 1, half)
            act(other, other * 2 + core)

    def all_of(ref, phase, count=half - 1):
        part = ref.at[pl.ds(0, count)]
        return remote(part, part, phase, partner)

    barrier = pltpu.get_barrier_semaphore()
    for i in range(1, n):
        pl.semaphore_signal(
            barrier,
            inc=1,
            device_id={"seq": lax.rem(me + i, n)},
            device_id_type=pl.DeviceIdType.MESH,
        )

    first, second = pl.ds(0, keys), pl.ds(keys, keys)
    wo_rows = pl.ds(pl.multiple_of(core * (slab // 2), slab // 2), slab // 2)
    sources = (aqkv_in, vqkv.at[1], vqkv.at[2], vqkv.at[0], wo, stream_in, gain_in, w1, w2)
    places = (
        aqkv, vk.at[first], vv.at[first], vq, wo_v.at[wo_rows],
        stream, gain, w1_v.at[core], w2_v.at[core],
    )
    loads = [
        pltpu.make_async_copy(src, dst, load_sem.at[i])
        for i, (src, dst) in enumerate(zip(sources, places))
    ]
    for load in loads:
        load.start()

    def own_blocks(value):
        for c in range(chunks):
            relay_own[pl.ds(c, tokens, stride=chunks), :] = value[:, c * LANES : (c + 1) * LANES]
        return relay_own[...]

    far = n // near
    my_far, my_near = lax.div(me, near), lax.rem(me, near)
    kv_slot = my_near * far + my_far
    kv_row = pl.ds(my_near * far, far)

    loads[0].wait()
    g_q[chip] = (own_blocks(aqkv[0].astype(F32)) * SCALE).astype(BF16)
    g_kv[kv_slot, 0:block] = (own_blocks(aqkv[1].astype(F32)) * SCALE).astype(BF16)
    g_kv[kv_slot, block : 2 * block] = own_blocks(aqkv[2].astype(F32)).astype(BF16)

    pl.semaphore_wait(barrier, n - 1)
    shared = [
        remote(vqkv.at[1], vk.at[second], 7, partner),
        remote(vqkv.at[2], vv.at[second], 8, partner),
        remote(wo, wo_v.at[wo_rows], 9, partner),
        remote(w1, w1_v.at[core], 10, partner),
        remote(w2, w2_v.at[core], 11, partner),
    ]
    each_chip(lambda other, peer: remote(g_q.at[chip], g_q.at[chip], 0, peer).start())
    for copy in shared[0:2]:
        copy.start()
    for i in range(1, far):
        peer = lax.rem(my_far + i, far) * near + my_near
        remote(g_kv.at[kv_slot], g_kv.at[kv_slot], 1, peer).start()

    def rows_of(blocks):
        step = chunks
        count = blocks.shape[0] * blocks.shape[1]
        relay[0:count] = blocks.astype(F32).reshape(count, LANES)
        return jnp.concatenate(
            [
                relay[pl.ds(c, count // step, stride=step), :].astype(BF16)
                for c in range(step)
            ],
            axis=1,
        )

    def blocks_of(value):
        for c in range(chunks):
            relay[pl.ds(c, asked, stride=chunks), :] = value[:, c * LANES : (c + 1) * LANES]
        return relay[0 : asked * chunks].astype(BF16).reshape(half, block, LANES)

    def scatter(value, send, recv, phase):
        send[...] = blocks_of(value)
        each_chip(lambda other, peer: remote(send.at[other], recv.at[chip], phase, peer).start())
        recv[chip] = send[chip]

    def gathered_sum(recv):
        return jnp.sum(recv[...].astype(F32), axis=0)

    def diagonal(part, sub, group):
        head = lane_of(part.shape) // HD
        return jnp.concatenate(
            [jnp.where(head == sub * group + h, part, jnp.zeros_like(part)) for h in range(group)],
            axis=0,
        )

    def windows_of(rows):
        group = LANES // rows
        window = max(group * HD, LANES)
        return group, window, width // window, window // (group * HD)

    group, window, windows, subs = windows_of(asked)
    receivers = half // (windows * subs)
    rows = HD // receivers

    loads[1].wait()
    loads[2].wait()
    def turn_values(part):
        for w in range(windows):
            cols = slice(w * window, (w + 1) * window)
            vt[cols, part] = vv[part, cols].T

    def score(part):
        for w in range(windows):
            cols = slice(w * window, (w + 1) * window)
            for sub in range(subs):
                spread = diagonal(qmat[:, cols], sub, group)
                logits[w * subs + sub, part] = mm(vk[part, cols], spread, 1, 1)

    own_part, other_part = slice(0, keys), slice(keys, 2 * keys)
    turn_values(own_part)
    all_of(g_q, 0).wait_recv()
    qmat[...] = rows_of(g_q[...])
    score(own_part)
    shared[0].wait_recv()
    score(other_part)
    statistics = []
    for at in range(windows * subs):
        scores = logits[at]
        peak = jnp.max(scores, axis=0, keepdims=True).astype(BF16).astype(F32)
        weights = jnp.exp(scores - peak)
        statistics.append((peak, jnp.sum(weights, axis=0, keepdims=True)))
        rounded[at] = weights.astype(BF16)
    shared[1].wait_recv()
    turn_values(other_part)

    for w in range(windows):
        cols = slice(w * window, (w + 1) * window)
        for sub in range(subs):
            peak, total = statistics[w * subs + sub]
            product = mm(vt[cols, :], rounded[w * subs + sub], 1, 0)
            lane = lane_of((HD, LANES)) // asked
            chosen = jnp.zeros((HD, LANES), F32)
            for h in range(group):
                at = (sub * group + h) * HD
                chosen = jnp.where(lane == h, product[at : at + HD], chosen)
            high = total.astype(BF16).astype(F32)
            row = lax.broadcasted_iota(jnp.int32, (STATS, LANES), 0)
            stats = jnp.where(
                row == 0, peak, jnp.where(row == 1, high, jnp.where(row == 2, total - high, 0.0))
            )
            for j in range(receivers):
                if slab < HD:
                    numerator, kept = chosen[j * rows : (j + 1) * rows], stats
                else:
                    span = slab // HD * asked
                    numerator, kept = jnp.zeros((rows, LANES), F32), jnp.zeros((STATS, LANES), F32)
                    for i in range(LANES // span):
                        shift = (i - j) * span % LANES
                        part, part_stats = chosen[i * rows : (i + 1) * rows], stats
                        if shift:
                            part = pltpu.roll(part, shift, 1)
                            part_stats = pltpu.roll(part_stats, shift, 1)
                        numerator = jnp.where(
                            lane_of((rows, LANES)) // span == i, part, numerator
                        )
                        kept = jnp.where(lane_of((STATS, LANES)) // span == i, part_stats, kept)
                target = (w * subs + sub) * receivers + j
                p_send[target, 0:rows] = numerator.astype(BF16)
                p_send[target, rows : rows + STATS] = kept.astype(BF16)

    each_chip(lambda other, peer: remote(p_send.at[other], p_recv.at[chip], 2, peer).start())
    all_of(g_kv, 1, far - 1).wait_recv()
    for i in range(1, near):
        peer = my_far * near + lax.rem(my_near + i, near)
        remote(g_kv.at[kv_row], g_kv.at[kv_row], 6, peer).start()
    for copy in shared[2:]:
        copy.start()
    p_recv[chip] = p_send[chip]

    store = pltpu.make_async_copy(vmix, vmix_out, out_sem)
    v_group, v_window, v_windows, v_subs = windows_of(audio)

    def video(start, stop):
        for w in range(start, stop):
            cols = slice(w * v_window, (w + 1) * v_window)
            mixed = None
            for sub in range(v_subs):
                scores = mm(diagonal(kmat[:, cols], sub, v_group), vq[:, cols], 1, 1)
                scores = scores.reshape(v_group, audio, scores.shape[1])
                weights = jnp.exp(scores - jnp.max(scores, axis=1, keepdims=True))
                weights = weights * (1.0 / jnp.sum(weights, axis=1, keepdims=True))
                weights = weights.reshape(v_group * audio, scores.shape[2])
                term = mm(weights.T.astype(BF16), diagonal(vmat[:, cols], sub, v_group), 1, 0)
                mixed = term if mixed is None else mixed + term
            vmix[:, cols] = mixed.astype(BF16)

    all_of(p_recv, 2).wait_recv()
    parts = p_recv[...].astype(F32)
    peaks = parts[:, rows : rows + 1]
    scales = jnp.exp(peaks - jnp.max(peaks, axis=0, keepdims=True))
    totals = (parts[:, rows + 1 : rows + 2] + parts[:, rows + 2 : rows + 3]) * scales
    attended = jnp.sum(parts[:, 0:rows] * scales, axis=0) / jnp.sum(totals, axis=0)
    turned = attended.T.astype(BF16)
    if slab < HD:
        columns = turned
    else:
        heads = slab // HD
        folds = HD // rows
        columns = jnp.concatenate(
            [
                turned[(f * heads + h) * asked : (f * heads + h + 1) * asked]
                for h in range(heads)
                for f in range(folds)
            ],
            axis=1,
        )

    loads[4].wait()
    shared[2].wait_recv()
    scatter(mm(columns, wo_v[...], 1, 0), a_send, a_recv, 3)
    loads[5].wait()
    loads[6].wait()
    own = own_blocks(stream[...].astype(F32))
    all_of(g_kv, 6, far * (near - 1)).wait_recv()
    loads[3].wait()
    kmat[...] = rows_of(g_kv[:, 0:block])
    vmat[...] = rows_of(g_kv[:, block : 2 * block])
    video(0, v_windows // 2)
    all_of(a_recv, 3).wait_recv()
    mixed_audio = own + gathered_sum(a_recv)

    by_token = mixed_audio.reshape(tokens, chunks, LANES)
    square = jnp.sum(jnp.sum(by_token * by_token, axis=1, keepdims=True), axis=2, keepdims=True)
    normed = by_token * lax.rsqrt(square / width + EPSILON) * gain[...][None]
    g_n[chip] = normed.reshape(block, LANES).astype(BF16)
    each_chip(lambda other, peer: remote(g_n.at[chip], g_n.at[chip], 4, peer).start())
    video(v_windows // 2, v_windows)
    store.start()
    loads[7].wait()
    loads[8].wait()
    shared[3].wait_recv()
    shared[4].wait_recv()
    all_of(g_n, 4).wait_recv()

    features = rows_of(g_n[...])
    part = None
    for k in range(2):
        hidden = jax.nn.gelu(mm(features, w1_v[k], 1, 0), approximate=True).astype(BF16)
        term = mm(hidden, w2_v[k], 1, 0)
        part = term if part is None else part + term
    scatter(part, o_send, o_recv, 5)
    all_of(o_recv, 5).wait_recv()
    relay_own[...] = mixed_audio + gathered_sum(o_recv)
    for c in range(chunks):
        result[:, c * LANES : (c + 1) * LANES] = relay_own[
            pl.ds(c, tokens, stride=chunks), :
        ].astype(BF16)

    for copy in shared:
        copy.wait_send()
    all_of(g_kv, 1, far - 1).wait_send()
    all_of(g_kv, 6, far * (near - 1)).wait_send()
    for phase, ref in ((0, g_q), (2, p_send), (3, a_send), (4, g_n), (5, o_send)):
        all_of(ref, phase).wait_send()
    store.wait()


def write_results(mixed, result, mixed_out, result_out, mixed_v, result_v, sem):
    size = mixed.shape[0] // PIECES
    moves = [(result, result_v, result_out)]
    for i in range(PIECES):
        rows = pl.ds(i * size, size)
        moves.append((mixed.at[rows], mixed_v.at[rows], mixed_out.at[rows]))
    reads = [pltpu.make_async_copy(a, b, sem.at[0, i]) for i, (a, b, _) in enumerate(moves)]
    writes = [pltpu.make_async_copy(b, c, sem.at[1, i]) for i, (_, b, c) in enumerate(moves)]
    for read in reads:
        read.start()
    for read, write in zip(reads, writes):
        read.wait()
        write.start()
    for write in writes:
        write.wait()


def local(n, audio_stream, audio_qkv, video_qkv, attention_out, norm_gain, weight_in, weight_out):
    tokens, width = audio_stream.shape
    chunks = width // LANES
    block = tokens * chunks
    audio = n * tokens
    video = video_qkv.shape[1]
    asked = audio // 2
    receivers = n // 2 * LANES // (asked * HEADS)
    part = HD // receivers + STATS
    hidden = weight_in.shape[1]
    slab = attention_out.shape[0]
    anywhere = pl.BlockSpec(memory_space=pltpu.HBM)
    vmem = pl.BlockSpec(memory_space=pltpu.VMEM)
    by_chip = pltpu.VMEM((n // 2, block, LANES), BF16)
    parts = pltpu.VMEM((n // 2, part, LANES), BF16)
    mixed, result = pl.pallas_call(
        functools.partial(kernel, n, math.gcd(n, NEAR)),
        out_shape=(
            jax.ShapeDtypeStruct((video, width), BF16),
            jax.ShapeDtypeStruct((tokens, width), BF16),
        ),
        in_specs=[anywhere] * 7,
        out_specs=(anywhere, vmem),
        scratch_shapes=[
            pltpu.VMEM(audio_stream.shape, BF16),
            pltpu.VMEM(audio_qkv.shape, BF16),
            pltpu.VMEM((chunks, LANES), F32),
            pltpu.VMEM((video, width), BF16),
            pltpu.VMEM((2 * video, width), BF16),
            pltpu.VMEM((2 * video, width), BF16),
            pltpu.VMEM((width, 2 * video), BF16),
            pltpu.VMEM((2 * slab, width), BF16),
            pltpu.VMEM((2, width, hidden), BF16),
            pltpu.VMEM((2, hidden, width), BF16),
            pltpu.VMEM((video, width), BF16),
            pltpu.VMEM((audio * chunks, LANES), F32),
            pltpu.VMEM((block, LANES), F32),
            pltpu.VMEM((asked, width), BF16),
            pltpu.VMEM((audio, width), BF16),
            pltpu.VMEM((audio, width), BF16),
            pltpu.VMEM((HEADS * asked // LANES, 2 * video, LANES), F32),
            pltpu.VMEM((HEADS * asked // LANES, 2 * video, LANES), BF16),
            by_chip,
            pltpu.VMEM((n, 2 * block, LANES), BF16),
            parts,
            parts,
            by_chip,
            by_chip,
            by_chip,
            by_chip,
            by_chip,
            pltpu.SemaphoreType.DMA((9,)),
            pltpu.SemaphoreType.DMA,
            pltpu.SemaphoreType.DMA((12,)),
            pltpu.SemaphoreType.DMA((12,)),
        ],
        compiler_params=pltpu.CompilerParams(
            collective_id=0, has_side_effects=True, vmem_limit_bytes=60 * 1024 * 1024
        ),
        name="cross_modal_layer",
    )(
        audio_stream,
        audio_qkv,
        video_qkv,
        attention_out,
        norm_gain.reshape(chunks, LANES),
        weight_in,
        weight_out,
    )
    return pl.pallas_call(
        write_results,
        out_shape=(
            jax.ShapeDtypeStruct(mixed.shape, BF16),
            jax.ShapeDtypeStruct(result.shape, BF16),
        ),
        in_specs=[anywhere] * 2,
        out_specs=(anywhere, anywhere),
        scratch_shapes=[
            pltpu.VMEM(mixed.shape, BF16),
            pltpu.VMEM(result.shape, BF16),
            pltpu.SemaphoreType.DMA((2, PIECES + 1)),
        ],
        compiler_params=pltpu.CompilerParams(vmem_limit_bytes=60 * 1024 * 1024),
        name="write_results",
    )(mixed, result)


def solution(mesh):
    placed = (
        P(("groups", "seq"), None),
        P(None, ("groups", "seq"), None),
        P(None, ("groups", "seq"), None),
        P("seq", None),
        P(),
        P(None, "seq"),
        P("seq", None),
    )
    return jax.shard_map(
        functools.partial(local, mesh.shape["seq"]),
        mesh=mesh,
        in_specs=placed,
        out_specs=(P(("groups", "seq"), None), P(("groups", "seq"), None)),
        check_vma=False,
    )
```

```python
import functools
import math

import jax
import jax.numpy as jnp
from jax import lax
from jax.experimental import pallas as pl
from jax.experimental.pallas import tpu as pltpu
from jax.sharding import PartitionSpec as P

HEADS = 32
HD = 64
LANES = 128
STATS = 16
NEAR = 4
PIECES = 4
EPSILON = 1e-06
SCALE = 1.0 / math.sqrt(HD)
F32 = jnp.float32
BF16 = jnp.bfloat16


def mm(a, b, ca, cb):
    return lax.dot_general(a, b, (((ca,), (cb,)), ((), ())), preferred_element_type=F32)


def lane_of(shape):
    return lax.broadcasted_iota(jnp.int32, shape, len(shape) - 1)


def kernel(
    n, near, stream_in, aqkv_in, vqkv, wo, gain_in, w1, w2,
    vmix_out, result,
    stream, aqkv, gain, vq, vk, vv, vt, wo_v, w1_v, w2_v, vmix,
    relay, relay_own, qmat, kmat, vmat, logits, rounded,
    g_q, g_kv, p_send, p_recv, a_send, a_recv, g_n, o_send, o_recv,
    load_sem, out_sem, send_sem, recv_sem,
):
    me = lax.axis_index("seq")
    core, chip = lax.rem(me, 2), lax.div(me, 2)
    partner = me + 1 - 2 * core
    half = n // 2
    tokens, width = stream_in.shape
    chunks = width // LANES
    block = tokens * chunks
    keys = vqkv.shape[1]
    units = w2.shape[0]
    slab = 2 * wo.shape[0]
    audio = n * tokens
    asked = half * tokens

    def remote(src, dst, phase, peer):
        return pltpu.make_async_remote_copy(
            src_ref=src,
            dst_ref=dst,
            send_sem=send_sem.at[phase],
            recv_sem=recv_sem.at[phase],
            device_id={"seq": peer},
            device_id_type=pl.DeviceIdType.MESH,
        )

    def each_chip(act):
        for i in range(1, half):
            other = lax.rem(chip + (i + half // 2 - 1) % (half - 1) + 1, half)
            act(other, other * 2 + core)

    def all_of(ref, phase, count=half - 1):
        part = ref.at[pl.ds(0, count)]
        return remote(part, part, phase, partner)

    barrier = pltpu.get_barrier_semaphore()
    for i in range(1, n):
        pl.semaphore_signal(
            barrier,
            inc=1,
            device_id={"seq": lax.rem(me + i, n)},
            device_id_type=pl.DeviceIdType.MESH,
        )

    first, second = pl.ds(0, keys), pl.ds(keys, keys)
    wo_rows = pl.ds(pl.multiple_of(core * (slab // 2), slab // 2), slab // 2)
    sources = (aqkv_in, vqkv.at[1], vqkv.at[2], vqkv.at[0], wo, stream_in, gain_in, w1, w2)
    places = (
        aqkv, vk.at[first], vv.at[first], vq, wo_v.at[wo_rows],
        stream, gain, w1_v.at[core], w2_v.at[core],
    )
    loads = [
        pltpu.make_async_copy(src, dst, load_sem.at[i])
        for i, (src, dst) in enumerate(zip(sources, places))
    ]
    for load in loads:
        load.start()

    def own_blocks(value):
        for c in range(chunks):
            relay_own[pl.ds(c, tokens, stride=chunks), :] = value[:, c * LANES : (c + 1) * LANES]
        return relay_own[...]

    far = n // near
    my_far, my_near = lax.div(me, near), lax.rem(me, near)
    kv_slot = my_near * far + my_far
    kv_row = pl.ds(my_near * far, far)

    loads[0].wait()
    g_q[chip] = (own_blocks(aqkv[0].astype(F32)) * SCALE).astype(BF16)
    g_kv[kv_slot, 0:block] = (own_blocks(aqkv[1].astype(F32)) * SCALE).astype(BF16)
    g_kv[kv_slot, block : 2 * block] = own_blocks(aqkv[2].astype(F32)).astype(BF16)

    pl.semaphore_wait(barrier, n - 1)
    shared = [
        remote(vqkv.at[1], vk.at[second], 7, partner),
        remote(vqkv.at[2], vv.at[second], 8, partner),
        remote(wo, wo_v.at[wo_rows], 9, partner),
        remote(w1, w1_v.at[core], 10, partner),
        remote(w2, w2_v.at[core], 11, partner),
    ]
    each_chip(lambda other, peer: remote(g_q.at[chip], g_q.at[chip], 0, peer).start())
    for copy in shared[0:2]:
        copy.start()
    for i in range(1, far):
        peer = lax.rem(my_far + i, far) * near + my_near
        remote(g_kv.at[kv_slot], g_kv.at[kv_slot], 1, peer).start()

    def rows_of(blocks):
        step = chunks
        count = blocks.shape[0] * blocks.shape[1]
        relay[0:count] = blocks.astype(F32).reshape(count, LANES)
        return jnp.concatenate(
            [
                relay[pl.ds(c, count // step, stride=step), :].astype(BF16)
                for c in range(step)
            ],
            axis=1,
        )

    def blocks_of(value):
        for c in range(chunks):
            relay[pl.ds(c, asked, stride=chunks), :] = value[:, c * LANES : (c + 1) * LANES]
        return relay[0 : asked * chunks].astype(BF16).reshape(half, block, LANES)

    def scatter(value, send, recv, phase):
        send[...] = blocks_of(value)
        each_chip(lambda other, peer: remote(send.at[other], recv.at[chip], phase, peer).start())
        recv[chip] = send[chip]

    def gathered_sum(recv):
        return jnp.sum(recv[...].astype(F32), axis=0)

    def diagonal(part, sub, group):
        head = lane_of(part.shape) // HD
        return jnp.concatenate(
            [jnp.where(head == sub * group + h, part, jnp.zeros_like(part)) for h in range(group)],
            axis=0,
        )

    def windows_of(rows):
        group = LANES // rows
        window = max(group * HD, LANES)
        return group, window, width // window, window // (group * HD)

    group, window, windows, subs = windows_of(asked)
    receivers = half // (windows * subs)
    rows = HD // receivers

    loads[1].wait()
    loads[2].wait()
    def turn_values(part):
        for w in range(windows):
            cols = slice(w * window, (w + 1) * window)
            vt[cols, part] = vv[part, cols].T

    def score(part):
        for w in range(windows):
            cols = slice(w * window, (w + 1) * window)
            for sub in range(subs):
                spread = diagonal(qmat[:, cols], sub, group)
                logits[w * subs + sub, part] = mm(vk[part, cols], spread, 1, 1)

    own_part, other_part = slice(0, keys), slice(keys, 2 * keys)
    turn_values(own_part)
    all_of(g_q, 0).wait_recv()
    qmat[...] = rows_of(g_q[...])
    score(own_part)
    shared[0].wait_recv()
    score(other_part)
    statistics = []
    for at in range(windows * subs):
        scores = logits[at]
        peak = jnp.max(scores, axis=0, keepdims=True).astype(BF16).astype(F32)
        weights = jnp.exp(scores - peak)
        statistics.append((peak, jnp.sum(weights, axis=0, keepdims=True)))
        rounded[at] = weights.astype(BF16)
    shared[1].wait_recv()
    turn_values(other_part)

    for w in range(windows):
        cols = slice(w * window, (w + 1) * window)
        for sub in range(subs):
            peak, total = statistics[w * subs + sub]
            product = mm(vt[cols, :], rounded[w * subs + sub], 1, 0)
            lane = lane_of((HD, LANES)) // asked
            chosen = jnp.zeros((HD, LANES), F32)
            for h in range(group):
                at = (sub * group + h) * HD
                chosen = jnp.where(lane == h, product[at : at + HD], chosen)
            high = total.astype(BF16).astype(F32)
            row = lax.broadcasted_iota(jnp.int32, (STATS, LANES), 0)
            stats = jnp.where(
                row == 0, peak, jnp.where(row == 1, high, jnp.where(row == 2, total - high, 0.0))
            )
            for j in range(receivers):
                if slab < HD:
                    numerator, kept = chosen[j * rows : (j + 1) * rows], stats
                else:
                    span = slab // HD * asked
                    numerator, kept = jnp.zeros((rows, LANES), F32), jnp.zeros((STATS, LANES), F32)
                    for i in range(LANES // span):
                        shift = (i - j) * span % LANES
                        part, part_stats = chosen[i * rows : (i + 1) * rows], stats
                        if shift:
                            part = pltpu.roll(part, shift, 1)
                            part_stats = pltpu.roll(part_stats, shift, 1)
                        numerator = jnp.where(
                            lane_of((rows, LANES)) // span == i, part, numerator
                        )
                        kept = jnp.where(lane_of((STATS, LANES)) // span == i, part_stats, kept)
                target = (w * subs + sub) * receivers + j
                p_send[target, 0:rows] = numerator.astype(BF16)
                p_send[target, rows : rows + STATS] = kept.astype(BF16)

    each_chip(lambda other, peer: remote(p_send.at[other], p_recv.at[chip], 2, peer).start())
    all_of(g_kv, 1, far - 1).wait_recv()
    for i in range(1, near):
        peer = my_far * near + lax.rem(my_near + i, near)
        remote(g_kv.at[kv_row], g_kv.at[kv_row], 6, peer).start()
    for copy in shared[2:]:
        copy.start()
    p_recv[chip] = p_send[chip]

    v_group, v_window, v_windows, v_subs = windows_of(audio)
    cuts = (0, v_windows // 4, 5 * v_windows // 8, v_windows)
    stores = []
    for i, (start, stop) in enumerate(((cuts[0], cuts[2]), (cuts[2], cuts[3]))):
        span = pl.ds(start * v_window, (stop - start) * v_window)
        stores.append(
            pltpu.make_async_copy(vmix.at[:, span], vmix_out.at[:, span], out_sem.at[i])
        )

    def video(start, stop):
        for w in range(start, stop):
            cols = slice(w * v_window, (w + 1) * v_window)
            mixed = None
            for sub in range(v_subs):
                scores = mm(diagonal(kmat[:, cols], sub, v_group), vq[:, cols], 1, 1)
                scores = scores.reshape(v_group, audio, scores.shape[1])
                weights = jnp.exp(scores - jnp.max(scores, axis=1, keepdims=True))
                weights = weights * (1.0 / jnp.sum(weights, axis=1, keepdims=True))
                weights = weights.reshape(v_group * audio, scores.shape[2])
                term = mm(weights.T.astype(BF16), diagonal(vmat[:, cols], sub, v_group), 1, 0)
                mixed = term if mixed is None else mixed + term
            vmix[:, cols] = mixed.astype(BF16)

    all_of(p_recv, 2).wait_recv()
    parts = p_recv[...].astype(F32)
    peaks = parts[:, rows : rows + 1]
    scales = jnp.exp(peaks - jnp.max(peaks, axis=0, keepdims=True))
    totals = (parts[:, rows + 1 : rows + 2] + parts[:, rows + 2 : rows + 3]) * scales
    attended = jnp.sum(parts[:, 0:rows] * scales, axis=0) / jnp.sum(totals, axis=0)
    turned = attended.T.astype(BF16)
    if slab < HD:
        columns = turned
    else:
        heads = slab // HD
        folds = HD // rows
        columns = jnp.concatenate(
            [
                turned[(f * heads + h) * asked : (f * heads + h + 1) * asked]
                for h in range(heads)
                for f in range(folds)
            ],
            axis=1,
        )

    loads[4].wait()
    shared[2].wait_recv()
    scatter(mm(columns, wo_v[...], 1, 0), a_send, a_recv, 3)
    loads[5].wait()
    loads[6].wait()
    own = own_blocks(stream[...].astype(F32))
    all_of(g_kv, 6, far * (near - 1)).wait_recv()
    loads[3].wait()
    kmat[...] = rows_of(g_kv[:, 0:block])
    vmat[...] = rows_of(g_kv[:, block : 2 * block])
    video(cuts[0], cuts[1])
    all_of(a_recv, 3).wait_recv()
    mixed_audio = own + gathered_sum(a_recv)

    by_token = mixed_audio.reshape(tokens, chunks, LANES)
    square = jnp.sum(jnp.sum(by_token * by_token, axis=1, keepdims=True), axis=2, keepdims=True)
    normed = by_token * lax.rsqrt(square / width + EPSILON) * gain[...][None]
    g_n[chip] = normed.reshape(block, LANES).astype(BF16)
    each_chip(lambda other, peer: remote(g_n.at[chip], g_n.at[chip], 4, peer).start())
    video(cuts[1], cuts[2])
    stores[0].start()
    loads[7].wait()
    loads[8].wait()
    shared[3].wait_recv()
    shared[4].wait_recv()
    all_of(g_n, 4).wait_recv()

    features = rows_of(g_n[...])
    part = None
    for k in range(2):
        hidden = jax.nn.gelu(mm(features, w1_v[k], 1, 0), approximate=True).astype(BF16)
        term = mm(hidden, w2_v[k], 1, 0)
        part = term if part is None else part + term
    scatter(part, o_send, o_recv, 5)
    video(cuts[2], cuts[3])
    stores[1].start()
    all_of(o_recv, 5).wait_recv()
    relay_own[...] = mixed_audio + gathered_sum(o_recv)
    for c in range(chunks):
        result[:, c * LANES : (c + 1) * LANES] = relay_own[
            pl.ds(c, tokens, stride=chunks), :
        ].astype(BF16)

    for copy in shared:
        copy.wait_send()
    all_of(g_kv, 1, far - 1).wait_send()
    all_of(g_kv, 6, far * (near - 1)).wait_send()
    for phase, ref in ((0, g_q), (2, p_send), (3, a_send), (4, g_n), (5, o_send)):
        all_of(ref, phase).wait_send()
    for store in stores:
        store.wait()


def write_results(mixed, result, mixed_out, result_out, mixed_v, result_v, sem):
    size = mixed.shape[0] // PIECES
    moves = [(result, result_v, result_out)]
    for i in range(PIECES):
        rows = pl.ds(i * size, size)
        moves.append((mixed.at[rows], mixed_v.at[rows], mixed_out.at[rows]))
    reads = [pltpu.make_async_copy(a, b, sem.at[0, i]) for i, (a, b, _) in enumerate(moves)]
    writes = [pltpu.make_async_copy(b, c, sem.at[1, i]) for i, (_, b, c) in enumerate(moves)]
    for read in reads:
        read.start()
    for read, write in zip(reads, writes):
        read.wait()
        write.start()
    for write in writes:
        write.wait()


def local(n, audio_stream, audio_qkv, video_qkv, attention_out, norm_gain, weight_in, weight_out):
    tokens, width = audio_stream.shape
    chunks = width // LANES
    block = tokens * chunks
    audio = n * tokens
    video = video_qkv.shape[1]
    asked = audio // 2
    receivers = n // 2 * LANES // (asked * HEADS)
    part = HD // receivers + STATS
    hidden = weight_in.shape[1]
    slab = attention_out.shape[0]
    anywhere = pl.BlockSpec(memory_space=pltpu.HBM)
    vmem = pl.BlockSpec(memory_space=pltpu.VMEM)
    by_chip = pltpu.VMEM((n // 2, block, LANES), BF16)
    parts = pltpu.VMEM((n // 2, part, LANES), BF16)
    mixed, result = pl.pallas_call(
        functools.partial(kernel, n, math.gcd(n, NEAR)),
        out_shape=(
            jax.ShapeDtypeStruct((video, width), BF16),
            jax.ShapeDtypeStruct((tokens, width), BF16),
        ),
        in_specs=[anywhere] * 7,
        out_specs=(anywhere, vmem),
        scratch_shapes=[
            pltpu.VMEM(audio_stream.shape, BF16),
            pltpu.VMEM(audio_qkv.shape, BF16),
            pltpu.VMEM((chunks, LANES), F32),
            pltpu.VMEM((video, width), BF16),
            pltpu.VMEM((2 * video, width), BF16),
            pltpu.VMEM((2 * video, width), BF16),
            pltpu.VMEM((width, 2 * video), BF16),
            pltpu.VMEM((2 * slab, width), BF16),
            pltpu.VMEM((2, width, hidden), BF16),
            pltpu.VMEM((2, hidden, width), BF16),
            pltpu.VMEM((video, width), BF16),
            pltpu.VMEM((audio * chunks, LANES), F32),
            pltpu.VMEM((block, LANES), F32),
            pltpu.VMEM((asked, width), BF16),
            pltpu.VMEM((audio, width), BF16),
            pltpu.VMEM((audio, width), BF16),
            pltpu.VMEM((HEADS * asked // LANES, 2 * video, LANES), F32),
            pltpu.VMEM((HEADS * asked // LANES, 2 * video, LANES), BF16),
            by_chip,
            pltpu.VMEM((n, 2 * block, LANES), BF16),
            parts,
            parts,
            by_chip,
            by_chip,
            by_chip,
            by_chip,
            by_chip,
            pltpu.SemaphoreType.DMA((9,)),
            pltpu.SemaphoreType.DMA((2,)),
            pltpu.SemaphoreType.DMA((12,)),
            pltpu.SemaphoreType.DMA((12,)),
        ],
        compiler_params=pltpu.CompilerParams(
            collective_id=0, has_side_effects=True, vmem_limit_bytes=60 * 1024 * 1024
        ),
        name="cross_modal_layer",
    )(
        audio_stream,
        audio_qkv,
        video_qkv,
        attention_out,
        norm_gain.reshape(chunks, LANES),
        weight_in,
        weight_out,
    )
    return pl.pallas_call(
        write_results,
        out_shape=(
            jax.ShapeDtypeStruct(mixed.shape, BF16),
            jax.ShapeDtypeStruct(result.shape, BF16),
        ),
        in_specs=[anywhere] * 2,
        out_specs=(anywhere, anywhere),
        scratch_shapes=[
            pltpu.VMEM(mixed.shape, BF16),
            pltpu.VMEM(result.shape, BF16),
            pltpu.SemaphoreType.DMA((2, PIECES + 1)),
        ],
        compiler_params=pltpu.CompilerParams(vmem_limit_bytes=60 * 1024 * 1024),
        name="write_results",
    )(mixed, result)


def solution(mesh):
    placed = (
        P(("groups", "seq"), None),
        P(None, ("groups", "seq"), None),
        P(None, ("groups", "seq"), None),
        P("seq", None),
        P(),
        P(None, "seq"),
        P("seq", None),
    )
    return jax.shard_map(
        functools.partial(local, mesh.shape["seq"]),
        mesh=mesh,
        in_specs=placed,
        out_specs=(P(("groups", "seq"), None), P(("groups", "seq"), None)),
        check_vma=False,
    )
```
